32 devices in a mesh: section: 2 (over core), fsdp: 16 (over z, y, x).
Axes of the slice: x: 2, y: 2, z: 4, core: 2. Of those that a mesh axis runs over, the one named last changes fastest.
Arguments:
- inputs: bfloat16 [2, 2048, 1600], P(None, 'fsdp'), may hold values from -6 to 6
- cotangent: bfloat16 [2, 2048, 1600], P(None, 'fsdp'), may hold values from -6 to 6
- segments: int32 [2, 2048], P(None, 'fsdp'), may hold values from 0 to 5, as said below
- ln1_gain: bfloat16 [2, 1600], P('section', 'fsdp'), may hold values from 0.5 to 1.5
- ln1_bias: bfloat16 [2, 1600], P('section', 'fsdp'), may hold values from -1.25 to 1.25
- w_qkv: bfloat16 [2, 1600, 4800], P('section', 'fsdp'), may hold values from -0.15625 to 0.15625
- b_qv: bfloat16 [2, 3200], P('section', 'fsdp'), may hold values from -1.25 to 1.25
- w_out: bfloat16 [2, 1600, 1600], P('section', 'fsdp'), may hold values from -1.75 to 1.75
- b_out: bfloat16 [2, 1600], P('section', 'fsdp'), may hold values from -1.25 to 1.25
- ln2_gain: bfloat16 [2, 1600], P('section', 'fsdp'), may hold values from 0.5 to 1.5
- ln2_bias: bfloat16 [2, 1600], P('section', 'fsdp'), may hold values from -1.25 to 1.25
- w_fc: bfloat16 [2, 1600, 6400], P('section', 'fsdp'), may hold values from -0.15625 to 0.15625
- b_fc: bfloat16 [2, 6400], P('section', 'fsdp'), may hold values from -1.25 to 1.25
- w_proj: bfloat16 [2, 1600, 6400], P('section', 'fsdp'), may hold values from -0.078125 to 0.078125
- b_proj: bfloat16 [2, 1600], P('section', 'fsdp'), may hold values from -1.25 to 1.25
Outputs:
- activations: bfloat16 [2, 2, 2048, 1600], P('section', None, 'fsdp')
- input_grad: bfloat16 [2, 2, 2048, 1600], P('section', None, 'fsdp')
- grad_ln1_gain: float32 [2, 1600], P('section', 'fsdp')
- grad_ln1_bias: float32 [2, 1600], P('section', 'fsdp')
- grad_w_qkv: float32 [2, 1600, 4800], P('section', 'fsdp')
- grad_b_qv: float32 [2, 3200], P('section', 'fsdp')
- grad_w_out: float32 [2, 1600, 1600], P('section', 'fsdp')
- grad_b_out: float32 [2, 1600], P('section', 'fsdp')
- grad_ln2_gain: float32 [2, 1600], P('section', 'fsdp')
- grad_ln2_bias: float32 [2, 1600], P('section', 'fsdp')
- grad_w_fc: float32 [2, 1600, 6400], P('section', 'fsdp')
- grad_b_fc: float32 [2, 6400], P('section', 'fsdp')
- grad_w_proj: float32 [2, 1600, 6400], P('section', 'fsdp')
- grad_b_proj: float32 [2, 1600], P('section', 'fsdp')
The draws below stay inside these ranges and needn't reach their ends.
Inputs may be any that keep to these rules, and one draw needn't show every extreme that they name: `segments`: in each micro-batch, pack k (tokens k * 1024 to (k + 1) * 1024 - 1) holds three documents numbered 3 k, 3 k + 1, 3 k + 2 in order; the middle one has exactly 800 tokens, the first and the last 60 or more; the first has fewer than 128 tokens and the last at most 128.
All inputs are finite; a program needn't handle non-finite values.
Results may differ from the reference program's by a relative error of at most 0.019.
Values may be sent and summed in bfloat16 or wider, within the bound.
No kernel may reach another device: no remote copies, remote signals or barrier semaphores. Data moves between devices by JAX's collectives and lax.ppermute only.
A program may use at most 576 MiB of HBM per device.

```python
import math
import jax
import jax.numpy as jnp
from jax import lax

D = 1600
HEADS = 25
HEAD_DIM = 64
FF = 6400
SEQ_LEN = 1024
TOK_DEV = 128
MICRO = 2
DOC_MAX = 800
DOC_MIN = 60
ROWS = 2048
N_SECTION = 2


def draw_segments(key, part):
    key = jax.random.fold_in(key, 11)
    seq_count = ROWS // SEQ_LEN
    lowest = max(DOC_MIN, SEQ_LEN - TOK_DEV - DOC_MAX + 1)
    highest = min(TOK_DEV - 1, SEQ_LEN - DOC_MAX - DOC_MIN)
    starts = jax.random.randint(key, (MICRO, seq_count, 1), lowest, highest + 1).astype(jnp.int32)
    positions = jnp.arange(SEQ_LEN, dtype=jnp.int32)[None, None, :]
    inside = (positions >= starts).astype(jnp.int32) + (positions >= starts + DOC_MAX).astype(jnp.int32)
    numbers = 3 * jnp.arange(seq_count, dtype=jnp.int32)[None, :, None] + inside
    return numbers.reshape(MICRO, ROWS).astype(jnp.int32)


def level_of(own_key, extent, pieces, least, largest):
    loudness, own = 1.0, jax.random.fold_in(own_key, 6)
    for dim, blocks in pieces:
        steps = jnp.exp(jax.random.uniform(jax.random.fold_in(own, dim), (blocks,), jnp.float32, least / len(pieces), largest / len(pieces)))
        loudness = loudness * jnp.repeat(steps, extent[dim] // blocks).reshape([-1 if axis == dim else 1 for axis in range(len(extent))])
    return loudness


def centred(own_key, shape, width, limit, split=(), held_as=jnp.bfloat16):
    factor_of = level_of(own_key, shape, split, -0.22, 0.18) if split else 1.0
    array = jax.random.normal(own_key, shape, jnp.float32) * width * factor_of
    return jnp.minimum(jnp.maximum(array, -limit), limit).astype(held_as)


def setup_inputs(seed: int = 0) -> dict:
    key_of = jax.random.split(jax.random.key(seed), 16)
    return {
        "inputs": centred(key_of[0], (MICRO, ROWS, D), 1.0, 6.0, ((1, 16),)),
        "cotangent": centred(key_of[1], (MICRO, ROWS, D), 1.0, 6.0, ((1, 16),)),
        "segments": draw_segments(jax.random.fold_in(key_of[15], 71), 0),
        "ln1_gain": jnp.clip(1.0 + 0.1 * jax.random.normal(key_of[3], (N_SECTION, D), jnp.float32), 0.5, 1.5).astype(jnp.bfloat16),
        "ln1_bias": centred(key_of[4], (N_SECTION, D), 0.2, 1.25, ((0, 2), (1, 16))),
        "w_qkv": centred(key_of[5], (N_SECTION, D, 3 * D), D ** -0.5, 0.15625, ((0, 2), (1, 16))),
        "b_qv": centred(key_of[6], (N_SECTION, 2 * D), 0.2, 1.25, ((0, 2), (1, 16))),
        "w_out": centred(key_of[7], (N_SECTION, D, D), (max(1, D * 8 // SEQ_LEN)) ** -0.5, 1.75, ((0, 2), (1, 16))),
        "b_out": centred(key_of[8], (N_SECTION, D), 0.2, 1.25, ((0, 2), (1, 16))),
        "ln2_gain": jnp.clip(1.0 + 0.1 * jax.random.normal(key_of[9], (N_SECTION, D), jnp.float32), 0.5, 1.5).astype(jnp.bfloat16),
        "ln2_bias": centred(key_of[10], (N_SECTION, D), 0.2, 1.25, ((0, 2), (1, 16))),
        "w_fc": centred(key_of[11], (N_SECTION, D, FF), D ** -0.5, 0.15625, ((0, 2), (1, 16))),
        "b_fc": centred(key_of[12], (N_SECTION, FF), 0.2, 1.25, ((0, 2), (1, 16))),
        "w_proj": centred(key_of[13], (N_SECTION, D, FF), FF ** -0.5, 0.078125, ((0, 2), (1, 16))),
        "b_proj": centred(key_of[14], (N_SECTION, D), 0.2, 1.25, ((0, 2), (1, 16))),
    }


@jax.custom_vjp
def low(v):
    return lax.optimization_barrier(v.astype(jnp.bfloat16)).astype(jnp.float32)

@jax.custom_vjp
def low_back(v):
    return v

def low_keep(v):
    return (low(v), None)

def low_pass(kept, grad):
    return (grad,)

def back_keep(v):
    return (v, None)

def back_low(kept, grad):
    return (low(grad),)
low.defvjp(low_keep, low_pass)
low_back.defvjp(back_keep, back_low)

def norm_rows(values, gain_vec, bias_vec):
    row_mean = lax.optimization_barrier(jnp.mean(values, axis=-1, keepdims=True))
    centered = values - row_mean
    variance = lax.optimization_barrier(jnp.mean(centered * centered, axis=-1, keepdims=True))
    return centered * lax.rsqrt(variance + 1e-05) * gain_vec + bias_vec

def matmul_high(left, right):
    return jnp.dot(left, right, precision=lax.Precision.HIGHEST)

def attend(queries, keys_all, values_all, segment_row):
    total_rows = queries.shape[0]
    seq_count = total_rows // SEQ_LEN
    score_scale = 1.0 / math.sqrt(HEAD_DIM)
    query_seqs = queries.reshape(seq_count, SEQ_LEN, HEADS, HEAD_DIM)
    key_seqs = keys_all.reshape(seq_count, SEQ_LEN, HEADS, HEAD_DIM)
    value_seqs = values_all.reshape(seq_count, SEQ_LEN, HEADS, HEAD_DIM)
    segment_seqs = segment_row.reshape(seq_count, SEQ_LEN)
    positions = jnp.arange(SEQ_LEN, dtype=jnp.int32)

    def one_sequence(packed):
        query_heads, key_heads, value_heads, segment_seq = packed
        scores = jnp.einsum('qhd,khd->hqk', query_heads, key_heads, precision=lax.Precision.HIGHEST) * score_scale
        scores = low_back(scores)
        allowed = (segment_seq[:, None] == segment_seq[None, :]) & (positions[None, :] <= positions[:, None])
        scores = jnp.where(allowed[None], scores, -1e+30)
        row_max = lax.optimization_barrier(jnp.max(scores, axis=-1, keepdims=True))
        exponent = jnp.exp(scores - row_max)
        attn_probs = low(exponent / lax.optimization_barrier(jnp.sum(exponent, axis=-1, keepdims=True)))
        return jnp.einsum('hqk,khd->qhd', attn_probs, value_heads, precision=lax.Precision.HIGHEST)
    context = lax.map(jax.checkpoint(one_sequence), (query_seqs, key_seqs, value_seqs, segment_seqs))
    return context.reshape(total_rows, HEADS * HEAD_DIM)

def layer(rows_all, params, segments):
    gain_one, bias_one, qkv_weight, qv_bias, out_weight, out_bias, gain_two, bias_two, fc_weight, fc_bias, proj_weight, proj_bias = params
    model_width = rows_all.shape[-1]
    qkv_bias = jnp.concatenate([qv_bias[:model_width], jnp.zeros((model_width,), qv_bias.dtype), qv_bias[model_width:]])
    outputs = []
    for micro_index in range(rows_all.shape[0]):
        rows_in = rows_all[micro_index]
        normed = low(norm_rows(rows_in, gain_one, bias_one))
        packed = low(low_back(matmul_high(normed, qkv_weight) + qkv_bias))
        queries = packed[:, :model_width]
        keys_part = packed[:, model_width:2 * model_width]
        values_part = packed[:, 2 * model_width:]
        context = low(low_back(attend(queries, keys_part, values_part, segments[micro_index])))
        middle = rows_in + low_back(matmul_high(context, out_weight) + out_bias)
        normed_two = low(norm_rows(middle, gain_two, bias_two))
        pre_act = low_back(matmul_high(normed_two, fc_weight) + fc_bias)
        activated = low(jax.nn.gelu(pre_act, approximate=True))
        outputs.append(middle + low_back(matmul_high(activated, proj_weight.T) + proj_bias))
    return jnp.stack(outputs)

def reference(inputs, cotangent, segments, ln1_gain, ln1_bias, w_qkv, b_qv, w_out, b_out, ln2_gain, ln2_bias, w_fc, b_fc, w_proj, b_proj):
    stacked = [weight.astype(jnp.float32) for weight in (ln1_gain, ln1_bias, w_qkv, b_qv, w_out, b_out, ln2_gain, ln2_bias, w_fc, b_fc, w_proj, b_proj)]
    rows_now = inputs.astype(jnp.float32)
    pullbacks = []
    section_outputs = []
    for section_index in range(N_SECTION):
        params = tuple((weight[section_index] for weight in stacked))
        result, pullback = jax.vjp(lambda rows_in, chosen: layer(rows_in, chosen, segments), rows_now, params)
        pullbacks.append(pullback)
        section_outputs.append(result.astype(jnp.bfloat16))
        rows_now = low(result)
    grad_now = cotangent.astype(jnp.float32)
    input_grads = [None] * N_SECTION
    weight_grads = [None] * N_SECTION
    for section_index in reversed(range(N_SECTION)):
        grad_rows, grad_params = pullbacks[section_index](grad_now)
        input_grads[section_index] = grad_rows.astype(jnp.bfloat16)
        weight_grads[section_index] = grad_params
        grad_now = low(grad_rows)
    stacked_grads = [jnp.stack([weight_grads[section_index][member] for section_index in range(N_SECTION)]) for member in range(12)]
    return (jnp.stack(section_outputs), jnp.stack(input_grads), stacked_grads[0], stacked_grads[1], stacked_grads[2], stacked_grads[3], stacked_grads[4], stacked_grads[5], stacked_grads[6], stacked_grads[7], stacked_grads[8], stacked_grads[9], stacked_grads[10], stacked_grads[11])
```

```python
import math

import jax
import jax.numpy as jnp
from jax import lax
from jax.experimental import pallas as pl
from jax.experimental.pallas import tpu as pltpu
from jax.sharding import PartitionSpec as P

HEADS = 25
HEAD_DIM = 64
SEQ_LEN = 1024
PACK_DEVS = 8
MAIN = HEADS // PACK_DEVS
SLOTS = 4
SLOT_COLS = SLOTS * HEAD_DIM
BLOCK = 256
BF = jnp.bfloat16
F32 = jnp.float32


def chip_swap(value, mask):
    count = lax.axis_size("fsdp")
    return lax.ppermute(value, "fsdp", [(i, i ^ mask) for i in range(count)])


def core_swap(value):
    return lax.ppermute(value, "section", [(0, 1), (1, 0)])


def ordered(bit, own, other, axis):
    return jnp.where(
        bit == 0,
        jnp.concatenate([own, other], axis=axis),
        jnp.concatenate([other, own], axis=axis),
    )


def take(value, index, size, axis):
    return lax.dynamic_slice_in_dim(value, index * size, size, axis)


def dot(left, right):
    return jnp.dot(left, right, preferred_element_type=F32)


def dot_rows(left, right):
    return lax.dot_general(left, right, (((0,), (0,)), ((), ())), preferred_element_type=F32)


def dot_cols(left, right):
    return lax.dot_general(left, right, (((1,), (1,)), ((), ())), preferred_element_type=F32)


def norm_rows(values, gain_vec, bias_vec):
    row_mean = jnp.mean(values, axis=-1, keepdims=True)
    centered = values - row_mean
    variance = jnp.mean(centered * centered, axis=-1, keepdims=True)
    return centered * lax.rsqrt(variance + 1e-05) * gain_vec + bias_vec


def gelu_tanh(values):
    return jax.nn.gelu(values, approximate=True)


def attend_kernel(q_ref, k_ref, v_ref, srow_ref, scol_ref, ctx_ref, p_ref, bias_ref):
    blocks = q_ref.shape[0] // BLOCK

    @pl.when(pl.program_id(0) == 0)
    def _():
        for i in range(blocks):
            rows = slice(i * BLOCK, (i + 1) * BLOCK)
            wide = (i + 1) * BLOCK
            r = lax.broadcasted_iota(jnp.int32, (BLOCK, wide), 0) + i * BLOCK
            c = lax.broadcasted_iota(jnp.int32, (BLOCK, wide), 1)
            same = scol_ref[rows, :] == srow_ref[:, :wide]
            bias_ref[rows, :wide] = jnp.where(same & (c <= r), 0.0, -1e30)

    for h in range(2):
        lanes = slice(h * HEAD_DIM, (h + 1) * HEAD_DIM)
        for i in range(blocks):
            rows = slice(i * BLOCK, (i + 1) * BLOCK)
            wide = (i + 1) * BLOCK
            q = q_ref[rows, lanes] * jnp.asarray(1.0 / math.sqrt(HEAD_DIM), BF)
            s = dot_cols(q, k_ref[:wide, lanes]) + bias_ref[rows, :wide]
            m = jnp.max(s, axis=-1, keepdims=True)
            e = jnp.exp(s - m)
            p = (e * (1.0 / jnp.sum(e, axis=-1, keepdims=True))).astype(BF)
            p_ref[h, rows, :wide] = p
            ctx_ref[rows, lanes] = dot(p, v_ref[:wide, lanes]).astype(BF)


def attend_back_kernel(q_ref, k_ref, v_ref, p_ref, d_ref, dq_ref, dk_ref, dv_ref, dk_sum, dv_sum):
    blocks = q_ref.shape[0] // BLOCK
    scale = jnp.asarray(1.0 / math.sqrt(HEAD_DIM), BF)
    for h in range(2):
        lanes = slice(h * HEAD_DIM, (h + 1) * HEAD_DIM)
        for i in reversed(range(blocks)):
            rows = slice(i * BLOCK, (i + 1) * BLOCK)
            wide = (i + 1) * BLOCK
            d = d_ref[rows, lanes]
            p_low = p_ref[h, rows, :wide]
            dp = dot_cols(d, v_ref[:wide, lanes])
            p = p_low.astype(F32)
            ds = (p * (dp - jnp.sum(p * dp, axis=-1, keepdims=True))).astype(BF)
            dq_ref[rows, lanes] = dot(ds, k_ref[:wide, lanes] * scale).astype(BF)
            dk = dot_rows(ds, q_ref[rows, lanes] * scale)
            dv = dot_rows(p_low, d)
            if i == blocks - 1:
                dk_sum[...] = dk
                dv_sum[...] = dv
            else:
                dk_sum[:wide, :] += dk
                dv_sum[:wide, :] += dv
        dk_ref[:, lanes] = dk_sum[...].astype(BF)
        dv_ref[:, lanes] = dv_sum[...].astype(BF)


def attend(packed, segs):
    length = packed.shape[0]
    pairs = SLOTS // 2
    lanes = 2 * HEAD_DIM
    return pl.pallas_call(
        attend_kernel,
        grid=(pairs,),
        in_specs=[
            pl.BlockSpec((length, lanes), lambda g: (0, g)),
            pl.BlockSpec((length, lanes), lambda g: (0, pairs + g)),
            pl.BlockSpec((length, lanes), lambda g: (0, 2 * pairs + g)),
            pl.BlockSpec((1, length), lambda g: (0, 0)),
            pl.BlockSpec((length, 1), lambda g: (0, 0)),
        ],
        out_specs=[
            pl.BlockSpec((length, lanes), lambda g: (0, g)),
            pl.BlockSpec((2, length, length), lambda g: (g, 0, 0)),
        ],
        out_shape=[
            jax.ShapeDtypeStruct((length, SLOT_COLS), BF),
            jax.ShapeDtypeStruct((SLOTS, length, length), BF),
        ],
        scratch_shapes=[pltpu.VMEM((length, length), F32)],
        compiler_params=pltpu.CompilerParams(vmem_limit_bytes=48 * 1024 * 1024),
        cost_estimate=pl.CostEstimate(flops=12 * 10**9, bytes_accessed=12 * 10**6, transcendentals=0),
    )(packed, packed, packed, segs.reshape(1, length), segs.reshape(length, 1))


def attend_back(packed, probs, grad):
    length = packed.shape[0]
    pairs = SLOTS // 2
    lanes = 2 * HEAD_DIM
    pair_block = pl.BlockSpec((length, lanes), lambda g: (0, g))
    return pl.pallas_call(
        attend_back_kernel,
        grid=(pairs,),
        in_specs=[
            pair_block,
            pl.BlockSpec((length, lanes), lambda g: (0, pairs + g)),
            pl.BlockSpec((length, lanes), lambda g: (0, 2 * pairs + g)),
            pl.BlockSpec((2, length, length), lambda g: (g, 0, 0)),
            pair_block,
        ],
        out_specs=[pair_block] * 3,
        out_shape=[jax.ShapeDtypeStruct((length, SLOT_COLS), BF)] * 3,
        scratch_shapes=[pltpu.VMEM((length, HEAD_DIM), F32)] * 2,
        compiler_params=pltpu.CompilerParams(vmem_limit_bytes=48 * 1024 * 1024),
        cost_estimate=pl.CostEstimate(flops=24 * 10**9, bytes_accessed=12 * 10**6, transcendentals=0),
    )(packed, packed, packed, probs, grad)


def to_slots(values):
    tokens = values.shape[0]
    split = PACK_DEVS * MAIN * HEAD_DIM
    main = values[:, :split].reshape(tokens, PACK_DEVS, MAIN * HEAD_DIM).transpose(1, 0, 2)
    last = values[None, :, split:]
    none = jnp.zeros((PACK_DEVS - 1,) + last.shape[1:], values.dtype)
    return jnp.concatenate([main, jnp.concatenate([last, none], axis=0)], axis=2)


def from_slots(slots):
    tokens = slots.shape[1]
    main = slots[:, :, : MAIN * HEAD_DIM].transpose(1, 0, 2).reshape(tokens, -1)
    return jnp.concatenate([main, slots[0, :, MAIN * HEAD_DIM :]], axis=1)


def pack_exchange(value):
    count = lax.axis_size("fsdp")
    groups = [list(range(first, first + PACK_DEVS)) for first in range(0, count, PACK_DEVS)]
    return lax.all_to_all(value, "fsdp", 0, 0, axis_index_groups=groups)


def gather_plane(quarter):
    half = quarter.shape[1] // 2
    by_x = chip_swap(quarter, 1)
    by_y = chip_swap(quarter, 2)
    left = chip_swap(by_x[:, :half], 2)
    right = chip_swap(by_y[:, half:], 1)
    return [quarter, by_x, by_y, jnp.concatenate([left, right], axis=1)]


def reduce_plane(parts):
    own, to_x, to_y, across = parts
    half = own.shape[1] // 2
    left = chip_swap(across[:, :half], 2)
    right = chip_swap(across[:, half:], 1)
    to_x = jnp.concatenate(
        [(to_x[:, :half].astype(F32) + left.astype(F32)).astype(BF), to_x[:, half:]], axis=1
    )
    to_y = jnp.concatenate(
        [to_y[:, :half], (to_y[:, half:].astype(F32) + right.astype(F32)).astype(BF)], axis=1
    )
    from_x = chip_swap(to_x, 1)
    from_y = chip_swap(to_y, 2)
    return own.astype(F32) + from_x.astype(F32) + from_y.astype(F32)


def bits_of(count):
    return count.bit_length() - 1


def gather_vector(value):
    index = lax.axis_index("fsdp")
    rows = value[None]
    for bit in range(bits_of(lax.axis_size("fsdp"))):
        rows = ordered((index >> bit) & 1, rows, chip_swap(rows, 1 << bit), 0)
    return rows


def reduce_vector(rows):
    index = lax.axis_index("fsdp")
    for bit in reversed(range(bits_of(lax.axis_size("fsdp")))):
        mine = (index >> bit) & 1
        half = rows.shape[0] // 2
        rows = take(rows, mine, half, 0) + chip_swap(take(rows, 1 - mine, half, 0), 1 << bit)
    return rows[0]


def on_device(
    inputs,
    cotangent,
    segments,
    ln1_gain,
    ln1_bias,
    w_qkv,
    b_qv,
    w_out,
    b_out,
    ln2_gain,
    ln2_bias,
    w_fc,
    b_fc,
    w_proj,
    b_proj,
):
    core = lax.axis_index("section")
    rank = lax.axis_index("fsdp")
    count = lax.axis_size("fsdp")
    bits = bits_of(count)
    tokens, width = inputs.shape[1:]
    shard = w_qkv.shape[1]
    hidden = w_fc.shape[2]
    quarter = width // 4
    high = count // 4
    pair_bit = (rank >> 2) & 1
    plane = rank & 3

    place = jnp.arange(width, dtype=jnp.int32)
    natural = ((place % quarter) // shard * 4 + ((place // quarter) ^ plane)) * shard + place % shard
    order = (jnp.arange(width, dtype=jnp.int32)[:, None] == natural[None, :]).astype(BF)

    def to_own(values):
        return dot(values, order).astype(BF)

    def to_natural(values):
        return dot_cols(values, order).astype(BF)

    def to_own_wide(values):
        top = values.astype(BF)
        return dot(top, order) + dot((values - top.astype(F32)).astype(BF), order)

    vectors = jnp.concatenate(
        [
            ln1_gain[0],
            ln1_bias[0],
            b_out[0],
            ln2_gain[0],
            ln2_bias[0],
            b_proj[0],
            b_qv[0],
            b_fc[0],
            lax.dynamic_index_in_dim(segments, core, 0, False).astype(BF),
        ]
    )
    vector_rows = gather_vector(vectors)
    segment_rows = vector_rows[:, 12 * shard :].astype(jnp.int32)
    pack_segments = take(segment_rows, rank // PACK_DEVS, PACK_DEVS, 0).reshape(-1)
    vector_rows = vector_rows[:, : 12 * shard]
    vector_other = core_swap(vector_rows)
    layer_vectors = []
    for layer in range(2):
        rows = jnp.where(core == layer, vector_rows, vector_other)
        model = jnp.stack([rows[:, i * shard : (i + 1) * shard].reshape(width) for i in range(6)])
        model = dot(model, order)
        qv = rows[:, 6 * shard : 8 * shard].reshape(2 * width).astype(F32)
        fc = rows[:, 8 * shard : 12 * shard].reshape(hidden).astype(F32)
        fc = lax.dynamic_slice_in_dim(fc, core * (hidden // 2) + pair_bit * (hidden // 4), hidden // 4, 0)
        qkv = jnp.concatenate([qv[:width], jnp.zeros((width,), F32), qv[width:]])
        layer_vectors.append((model, qkv, fc))

    def by_core(pieces):
        mine = jnp.concatenate([take(p, core, p.shape[1] // 2, 1) for p in pieces], axis=1)
        yours = jnp.concatenate([take(p, 1 - core, p.shape[1] // 2, 1) for p in pieces], axis=1)
        got = core_swap(yours)
        return [jnp.where(core == layer, mine, got) for layer in range(2)]

    def gather_high(rows, first_bit):
        for bit in range(first_bit, bits):
            rows = ordered((rank >> bit) & 1, rows, chip_swap(rows, 1 << bit), 0)
        return rows

    attn_shards = by_core([w_qkv[0], w_out[0]])
    mlp_shards = by_core([w_fc[0], w_proj[0]])

    def gather_attn(layer):
        rows = gather_high(attn_shards[layer][None], 2).reshape(quarter, -1)
        parts = gather_plane(rows)
        own = jnp.concatenate(parts, axis=0)
        other = jnp.concatenate([core_swap(part) for part in parts], axis=0)
        cut = w_qkv.shape[2] // 2
        return own[:, :cut], other[:, :cut], own[:, cut:], other[:, cut:]

    def gather_mlp(layer):
        both = mlp_shards[layer]
        half = hidden // 2
        small = hidden // 4
        fc_cols, proj_cols = both[:, :half], both[:, half:]
        mine = jnp.concatenate([take(fc_cols, pair_bit, small, 1), take(proj_cols, pair_bit, small, 1)], axis=1)
        yours = jnp.concatenate(
            [take(fc_cols, 1 - pair_bit, small, 1), take(proj_cols, 1 - pair_bit, small, 1)], axis=1
        )
        rows = ordered(pair_bit, mine[None], chip_swap(yours, 4)[None], 0)
        rows = gather_high(rows, 3).reshape(quarter, -1)
        full = jnp.concatenate(gather_plane(rows), axis=0)
        return full[:, :small], full[:, small:]

    attn_weights = [None, None]
    mlp_weights = [None, None]
    for layer in range(2):
        attn_weights[layer] = gather_attn(layer)
        mlp_weights[layer] = gather_mlp(layer)

    def halves(own, other):
        return ordered(core, own, other, 1)

    def gather_tokens(values):
        two = jnp.concatenate([values, chip_swap(values, 4)], axis=0)
        return jnp.concatenate([two, core_swap(two)], axis=0)

    def reduce_tokens(values):
        two = values[: 2 * tokens] + core_swap(values[2 * tokens :].astype(BF)).astype(F32)
        return two[:tokens] + chip_swap(two[tokens:].astype(BF), 4).astype(F32)

    def forward(layer, rows_in):
        model, qkv_bias, fc_bias = layer_vectors[layer]
        gain_one, bias_one, out_bias, gain_two, bias_two, proj_bias = [model[i] for i in range(6)]
        qkv_own, qkv_other, out_own, out_other = attn_weights[layer]
        fc_weight, proj_weight = mlp_weights[layer]
        normed_float, norm_back_one = jax.vjp(norm_rows, rows_in, gain_one, bias_one)
        normed = normed_float.astype(BF)
        packed = (halves(dot(normed, qkv_own), dot(normed, qkv_other)) + qkv_bias).astype(BF)
        sent = jnp.concatenate([to_slots(packed[:, i * width : (i + 1) * width]) for i in range(3)], axis=2)
        heads_packed = pack_exchange(sent).reshape(PACK_DEVS * tokens, -1)
        heads_ctx, probs = attend(heads_packed, pack_segments)
        context = from_slots(pack_exchange(heads_ctx.reshape(PACK_DEVS, tokens, -1)))
        context = to_own(context)
        attn_out = to_own_wide(halves(dot(context, out_own), dot(context, out_other)))
        middle = rows_in + attn_out + out_bias
        normed_two_float, norm_back_two = jax.vjp(norm_rows, middle, gain_two, bias_two)
        normed_two = gather_tokens(normed_two_float.astype(BF))
        pre_act = dot(normed_two, fc_weight) + fc_bias
        activated = gelu_tanh(pre_act).astype(BF)
        result = middle + reduce_tokens(dot_cols(activated, proj_weight)) + proj_bias
        kept = (norm_back_one, normed, heads_packed, probs, context, norm_back_two, normed_two, pre_act, activated)
        return result, kept

    def plane_terms(rows, columns):
        return [dot_rows(rows[:, k * quarter : (k + 1) * quarter], columns).astype(BF) for k in range(4)]

    def reduce_high(total, last_bit):
        for bit in reversed(range(last_bit, bits)):
            mine = (rank >> bit) & 1
            half = total.shape[0] // 2
            sent = take(total, 1 - mine, half, 0).astype(BF)
            total = take(total, mine, half, 0) + chip_swap(sent, 1 << bit).astype(F32)
        return total

    def backward(layer, upstream, kept):
        norm_back_one, normed, heads_packed, probs, context, norm_back_two, normed_two, pre_act, activated = kept
        qkv_own, qkv_other, out_own, out_other = attn_weights[layer]
        fc_weight, proj_weight = mlp_weights[layer]
        grad_out_low = upstream.astype(BF)
        grad_out_all = gather_tokens(grad_out_low)
        grad_act = dot(grad_out_all, proj_weight)
        gelu_back = jax.vjp(gelu_tanh, pre_act)[1]
        grad_pre = gelu_back(grad_act)[0].astype(BF)
        grad_norm_two = reduce_tokens(dot_cols(grad_pre, fc_weight))
        terms = [
            jnp.concatenate(pair, axis=1)
            for pair in zip(plane_terms(normed_two, grad_pre), plane_terms(grad_out_all, activated))
        ]
        total = reduce_high(reduce_plane(terms).reshape(high, shard, -1), 3)
        small = hidden // 4
        mine = take(total, pair_bit, 1, 0)[0]
        yours = chip_swap(take(total, 1 - pair_bit, 1, 0)[0].astype(BF), 4).astype(F32)
        grad_fc = ordered(pair_bit, mine[:, :small], yours[:, :small], 1)
        grad_proj = ordered(pair_bit, mine[:, small:], yours[:, small:], 1)

        grad_middle_norm, grad_gain_two, grad_bias_two = norm_back_two(grad_norm_two)
        grad_middle = upstream + grad_middle_norm
        grad_attn_own = grad_middle.astype(BF)
        grad_attn = to_natural(grad_attn_own)
        out_half = width // 2
        attn_mine = take(grad_attn, core, out_half, 1)
        attn_yours = take(grad_attn, 1 - core, out_half, 1)
        grad_context = (dot_cols(attn_mine, out_own) + dot_cols(attn_yours, out_other)).astype(BF)
        heads_grad = pack_exchange(to_slots(to_natural(grad_context))).reshape(PACK_DEVS * tokens, -1)
        heads_back = attend_back(heads_packed, probs, heads_grad)
        back = pack_exchange(jnp.concatenate(heads_back, axis=1).reshape(PACK_DEVS, tokens, -1))
        grad_packed = jnp.concatenate(
            [from_slots(back[:, :, i * SLOT_COLS : (i + 1) * SLOT_COLS]) for i in range(3)], axis=1
        )
        qkv_half = 3 * width // 2
        packed_mine = take(grad_packed, core, qkv_half, 1)
        packed_yours = take(grad_packed, 1 - core, qkv_half, 1)
        grad_normed = dot_cols(packed_mine, qkv_own) + dot_cols(packed_yours, qkv_other)
        grad_rows_norm, grad_gain_one, grad_bias_one = norm_back_one(grad_normed)
        grad_rows = grad_middle + grad_rows_norm
        got = core_swap(jnp.concatenate([normed, context, packed_yours, attn_yours], axis=1))
        normed_both = jnp.concatenate([normed, got[:, :width]], axis=0)
        context_both = jnp.concatenate([context, got[:, width : 2 * width]], axis=0)
        packed_both = jnp.concatenate([packed_mine, got[:, 2 * width : 2 * width + qkv_half]], axis=0)
        attn_both = jnp.concatenate([attn_mine, got[:, 2 * width + qkv_half :]], axis=0)
        terms = [
            jnp.concatenate(pair, axis=1)
            for pair in zip(plane_terms(normed_both, packed_both), plane_terms(context_both, attn_both))
        ]
        grad_attn_weights = reduce_high(reduce_plane(terms).reshape(high, shard, -1), 2)[0]
        model = jnp.stack(
            [
                grad_gain_one,
                grad_bias_one,
                jnp.sum(grad_attn_own.astype(F32), axis=0),
                grad_gain_two,
                grad_bias_two,
                jnp.sum(grad_out_low.astype(F32), axis=0),
            ]
        )
        model = lax.dot_general(
            model,
            order.astype(F32),
            (((1,), (1,)), ((), ())),
            precision=lax.Precision.HIGHEST,
            preferred_element_type=F32,
        )
        packed_float = grad_packed.astype(F32)
        qv = jnp.concatenate([jnp.sum(packed_float[:, :width], axis=0), jnp.sum(packed_float[:, 2 * width :], axis=0)])
        fc = lax.dynamic_update_slice_in_dim(
            jnp.zeros((hidden,), F32),
            jnp.sum(grad_pre.astype(F32), axis=0),
            core * (hidden // 2) + pair_bit * small,
            0,
        )
        vector_rows = jnp.concatenate(
            [model[i].reshape(count, shard) for i in range(6)]
            + [qv.reshape(count, 2 * shard), fc.reshape(count, 4 * shard)],
            axis=1,
        )
        return grad_rows, vector_rows, (grad_attn_weights[:, :qkv_half], grad_attn_weights[:, qkv_half:], grad_fc, grad_proj)

    own_inputs = lax.dynamic_index_in_dim(inputs, core, 0, False)
    own_cotangent = lax.dynamic_index_in_dim(cotangent, core, 0, False)
    first_out, first_kept = forward(0, to_own(own_inputs).astype(F32))
    first_low = first_out.astype(BF)
    second_out, second_kept = forward(1, first_low.astype(F32))
    second_low = second_out.astype(BF)
    second_grad, second_vectors, second_mats = backward(1, to_own(own_cotangent).astype(F32), second_kept)
    second_grad_low = second_grad.astype(BF)
    first_grad, first_vectors, first_mats = backward(0, second_grad_low.astype(F32), first_kept)
    first_grad_low = first_grad.astype(BF)

    def by_section(first, second):
        own = jnp.where(core == 0, first, second)
        got = core_swap(jnp.where(core == 0, second, first))
        return ordered(core, own[None], got[None], 0)

    section_outputs = by_section(to_natural(first_low), to_natural(second_low))
    input_grads = by_section(to_natural(first_grad_low), to_natural(second_grad_low))

    mats = []
    for first, second in zip(first_mats, second_mats):
        own = jnp.where(core == 0, first, second)
        got = core_swap(jnp.where(core == 0, second, first))
        mats.append(ordered(core, own, got, 1))
    vector_rows = jnp.where(core == 0, first_vectors, second_vectors) + core_swap(
        jnp.where(core == 0, second_vectors, first_vectors)
    )
    vector_own = reduce_vector(vector_rows)
    model = [vector_own[i * shard : (i + 1) * shard] for i in range(6)]
    return (
        section_outputs[None],
        input_grads[None],
        model[0][None],
        model[1][None],
        mats[0][None],
        vector_own[6 * shard : 8 * shard][None],
        mats[1][None],
        model[2][None],
        model[3][None],
        model[4][None],
        mats[2][None],
        vector_own[8 * shard :][None],
        mats[3][None],
        model[5][None],
    )


def solution(mesh):
    in_specs = (
        P(None, "fsdp", None),
        P(None, "fsdp", None),
        P(None, "fsdp"),
        P("section", "fsdp"),
        P("section", "fsdp"),
        P("section", "fsdp", None),
        P("section", "fsdp"),
        P("section", "fsdp", None),
        P("section", "fsdp"),
        P("section", "fsdp"),
        P("section", "fsdp"),
        P("section", "fsdp", None),
        P("section", "fsdp"),
        P("section", "fsdp", None),
        P("section", "fsdp"),
    )
    out_specs = (
        P("section", None, "fsdp", None),
        P("section", None, "fsdp", None),
        P("section", "fsdp"),
        P("section", "fsdp"),
        P("section", "fsdp", None),
        P("section", "fsdp"),
        P("section", "fsdp", None),
        P("section", "fsdp"),
        P("section", "fsdp"),
        P("section", "fsdp"),
        P("section", "fsdp", None),
        P("section", "fsdp"),
        P("section", "fsdp", None),
        P("section", "fsdp"),
    )
    return jax.shard_map(
        on_device, mesh=mesh, in_specs=in_specs, out_specs=out_specs, check_vma=False
    )
```

```python
import math

import jax
import jax.numpy as jnp
from jax import lax
from jax.experimental import pallas as pl
from jax.experimental.pallas import tpu as pltpu
from jax.sharding import PartitionSpec as P

HEADS = 25
HEAD_DIM = 64
SEQ_LEN = 1024
PACK_DEVS = 8
MAIN = HEADS // PACK_DEVS
SLOTS = 4
SLOT_COLS = SLOTS * HEAD_DIM
BLOCK = 256
BF = jnp.bfloat16
F32 = jnp.float32


def chip_swap(value, mask):
    count = lax.axis_size("fsdp")
    return lax.ppermute(value, "fsdp", [(i, i ^ mask) for i in range(count)])


def core_swap(value):
    return lax.ppermute(value, "section", [(0, 1), (1, 0)])


def fence(*values):
    return lax.optimization_barrier(values)


def ordered(bit, own, other, axis):
    return jnp.where(
        bit == 0,
        jnp.concatenate([own, other], axis=axis),
        jnp.concatenate([other, own], axis=axis),
    )


def take(value, index, size, axis):
    return lax.dynamic_slice_in_dim(value, index * size, size, axis)


def dot(left, right):
    return jnp.dot(left, right, preferred_element_type=F32)


def dot_rows(left, right):
    return lax.dot_general(left, right, (((0,), (0,)), ((), ())), preferred_element_type=F32)


def dot_cols(left, right):
    return lax.dot_general(left, right, (((1,), (1,)), ((), ())), preferred_element_type=F32)


def norm_rows(values, gain_vec, bias_vec):
    row_mean = jnp.mean(values, axis=-1, keepdims=True)
    centered = values - row_mean
    variance = jnp.mean(centered * centered, axis=-1, keepdims=True)
    return centered * lax.rsqrt(variance + 1e-05) * gain_vec + bias_vec


def gelu_tanh(values):
    return jax.nn.gelu(values, approximate=True)


def tokens_of(ref, first_row, blocks):
    rows = slice(first_row, first_row + HEAD_DIM)
    return jnp.concatenate([ref[s, rows, :] for s in range(blocks)], axis=1)


def attend_kernel(q_ref, k_ref, v_ref, srow_ref, scol_ref, ctx_ref, p_ref, bias_ref):
    per = q_ref.shape[2]
    length = q_ref.shape[0] * per
    step = BLOCK // per

    @pl.when(pl.program_id(0) == 0)
    def _():
        for first in range(0, length, BLOCK):
            wide = first + BLOCK
            key = lax.broadcasted_iota(jnp.int32, (wide, BLOCK), 0)
            query = lax.broadcasted_iota(jnp.int32, (wide, BLOCK), 1) + first
            same = scol_ref[:wide, :] == srow_ref[:, first:wide]
            bias_ref[:wide, first:wide] = jnp.where(same & (key <= query), 0.0, -1e30)

    for h in range(2):
        row = h * HEAD_DIM
        keys = tokens_of(k_ref, row, length // per)
        values = tokens_of(v_ref, row, length // per)
        queries = tokens_of(q_ref, row, length // per) * jnp.asarray(1.0 / math.sqrt(HEAD_DIM), BF)
        for first in range(0, length, BLOCK):
            wide = first + BLOCK
            s = dot_rows(keys[:, :wide], queries[:, first:wide]) + bias_ref[:wide, first:wide]
            m = jnp.max(s, axis=0, keepdims=True)
            e = jnp.exp(s - m)
            p = (e * (1.0 / jnp.sum(e, axis=0, keepdims=True))).astype(BF)
            p_ref[h, :wide, first:wide] = p
            ctx = dot(values[:, :wide], p).astype(BF)
            for i in range(step):
                ctx_ref[first // per + i, row : row + HEAD_DIM, :] = ctx[:, i * per : (i + 1) * per]


def attend_back_kernel(q_ref, k_ref, v_ref, p_ref, d_ref, back_ref, dk_sum, dv_sum):
    per = q_ref.shape[2]
    length = q_ref.shape[0] * per
    step = BLOCK // per
    scale = jnp.asarray(1.0 / math.sqrt(HEAD_DIM), BF)
    for h in range(2):
        row = h * HEAD_DIM
        rows = slice(row, row + HEAD_DIM)
        keys = tokens_of(k_ref, row, length // per) * scale
        values = tokens_of(v_ref, row, length // per)
        queries = tokens_of(q_ref, row, length // per) * scale
        grads = tokens_of(d_ref, row, length // per)
        for first in reversed(range(0, length, BLOCK)):
            wide = first + BLOCK
            d = grads[:, first:wide]
            p_low = p_ref[h, :wide, first:wide]
            dp = dot_rows(values[:, :wide], d)
            p = p_low.astype(F32)
            ds = (p * (dp - jnp.sum(p * dp, axis=0, keepdims=True))).astype(BF)
            dq = dot(keys[:, :wide], ds).astype(BF)
            for i in range(step):
                back_ref[first // per + i, 0, rows, :] = dq[:, i * per : (i + 1) * per]
            dk = dot_cols(queries[:, first:wide], ds)
            dv = dot_cols(d, p_low)
            if wide == length:
                dk_sum[...] = dk
                dv_sum[...] = dv
            else:
                dk_sum[:, :wide] += dk
                dv_sum[:, :wide] += dv
        for s in range(length // per):
            back_ref[s, 1, rows, :] = dk_sum[:, s * per : (s + 1) * per].astype(BF)
            back_ref[s, 2, rows, :] = dv_sum[:, s * per : (s + 1) * per].astype(BF)


def attend(packed, segs):
    devices, _, per = packed.shape
    length = devices * per
    pairs = SLOTS // 2
    rows = 2 * HEAD_DIM
    return pl.pallas_call(
        attend_kernel,
        grid=(pairs,),
        in_specs=[
            pl.BlockSpec((devices, rows, per), lambda g: (0, g, 0)),
            pl.BlockSpec((devices, rows, per), lambda g: (0, pairs + g, 0)),
            pl.BlockSpec((devices, rows, per), lambda g: (0, 2 * pairs + g, 0)),
            pl.BlockSpec((1, length), lambda g: (0, 0)),
            pl.BlockSpec((length, 1), lambda g: (0, 0)),
        ],
        out_specs=[
            pl.BlockSpec((devices, rows, per), lambda g: (0, g, 0)),
            pl.BlockSpec((2, length, length), lambda g: (g, 0, 0)),
        ],
        out_shape=[
            jax.ShapeDtypeStruct((devices, SLOT_COLS, per), BF),
            jax.ShapeDtypeStruct((SLOTS, length, length), BF),
        ],
        scratch_shapes=[pltpu.VMEM((length, length), F32)],
        compiler_params=pltpu.CompilerParams(vmem_limit_bytes=48 * 1024 * 1024),
        cost_estimate=pl.CostEstimate(flops=12 * 10**9, bytes_accessed=12 * 10**6, transcendentals=0),
    )(packed, packed, packed, segs.reshape(1, length), segs.reshape(length, 1))


def attend_back(packed, probs, grad):
    devices, _, per = packed.shape
    length = devices * per
    pairs = SLOTS // 2
    rows = 2 * HEAD_DIM
    pair_block = pl.BlockSpec((devices, rows, per), lambda g: (0, g, 0))
    back = pl.pallas_call(
        attend_back_kernel,
        grid=(pairs,),
        in_specs=[
            pair_block,
            pl.BlockSpec((devices, rows, per), lambda g: (0, pairs + g, 0)),
            pl.BlockSpec((devices, rows, per), lambda g: (0, 2 * pairs + g, 0)),
            pl.BlockSpec((2, length, length), lambda g: (g, 0, 0)),
            pair_block,
        ],
        out_specs=pl.BlockSpec((devices, 3, rows, per), lambda g: (0, 0, g, 0)),
        out_shape=jax.ShapeDtypeStruct((devices, 3, SLOT_COLS, per), BF),
        scratch_shapes=[pltpu.VMEM((HEAD_DIM, length), F32)] * 2,
        compiler_params=pltpu.CompilerParams(vmem_limit_bytes=48 * 1024 * 1024),
        cost_estimate=pl.CostEstimate(flops=24 * 10**9, bytes_accessed=12 * 10**6, transcendentals=0),
    )(packed, packed, packed, probs, grad)
    return back.reshape(devices, 3 * SLOT_COLS, per)


def to_slots(values):
    split = PACK_DEVS * MAIN * HEAD_DIM
    main = values[:split].reshape(PACK_DEVS, MAIN * HEAD_DIM, -1)
    last = values[None, split:]
    none = jnp.zeros((PACK_DEVS - 1,) + last.shape[1:], values.dtype)
    return jnp.concatenate([main, jnp.concatenate([last, none], axis=0)], axis=1)


def from_slots(slots):
    main = slots[:, : MAIN * HEAD_DIM].reshape(PACK_DEVS * MAIN * HEAD_DIM, -1)
    return jnp.concatenate([main, slots[0, MAIN * HEAD_DIM :]], axis=0)


def pack_exchange(value):
    count = lax.axis_size("fsdp")
    groups = [list(range(first, first + PACK_DEVS)) for first in range(0, count, PACK_DEVS)]
    return lax.all_to_all(value, "fsdp", 0, 0, axis_index_groups=groups)


def plane_first(quarter):
    return chip_swap(quarter, 1), chip_swap(quarter, 2)


def plane_second(got):
    return chip_swap(got[0][0], 2), chip_swap(got[1][1], 1)


def plane_whole(quarter, got, across):
    return tuple(jnp.concatenate([quarter[i], got[0][i], got[1][i], across[i]], axis=0) for i in range(2))


def sum_first(left, right):
    return chip_swap(left[3], 2), chip_swap(right[3], 1), chip_swap(left[2], 2), chip_swap(right[1], 1)


def sum_second(left, right, got):
    to_x = (left[1].astype(F32) + got[0].astype(F32)).astype(BF)
    to_y = (right[2].astype(F32) + got[1].astype(F32)).astype(BF)
    return chip_swap(to_x, 1), chip_swap(to_y, 2)


def sum_whole(left, right, got, last):
    left = left[0].astype(F32) + got[2].astype(F32) + last[0].astype(F32)
    right = right[0].astype(F32) + got[3].astype(F32) + last[1].astype(F32)
    return left.astype(BF), right.astype(BF)


def bits_of(count):
    return count.bit_length() - 1


def gather_bit(rows, bit):
    return ordered((lax.axis_index("fsdp") >> bit) & 1, rows, chip_swap(rows, 1 << bit), 0)


def reduce_vector(rows):
    index = lax.axis_index("fsdp")
    for bit in range(bits_of(lax.axis_size("fsdp"))):
        split = rows.reshape(-1, 2, rows.shape[-1])
        mine = (index >> bit) & 1
        rows = take(split, mine, 1, 1) + chip_swap(take(split, 1 - mine, 1, 1), 1 << bit)
        rows = rows[:, 0]
    return rows[0]


def on_device(
    inputs,
    cotangent,
    segments,
    ln1_gain,
    ln1_bias,
    w_qkv,
    b_qv,
    w_out,
    b_out,
    ln2_gain,
    ln2_bias,
    w_fc,
    b_fc,
    w_proj,
    b_proj,
):
    core = lax.axis_index("section")
    rank = lax.axis_index("fsdp")
    count = lax.axis_size("fsdp")
    bits = bits_of(count)
    tokens, width = inputs.shape[1:]
    shard = w_qkv.shape[1]
    hidden = w_fc.shape[2]
    quarter = width // 4
    pair_bit = (rank >> 2) & 1
    plane = rank & 3

    lines = count // 8

    place = jnp.arange(width, dtype=jnp.int32)
    block = place // shard
    line = block % (2 * lines)
    natural_line = ((((rank >> 3) ^ (line >> 1)) << 1) | (line & 1)) * 4 + ((place // quarter) ^ plane)
    natural_line = natural_line * shard + place % shard
    natural_side = (((block >> 3) * 2 + (block & 1)) * 4 + ((block >> 1) & 3)) * shard + place % shard

    def reorder(values, order):
        return dot(values, order).astype(BF)

    def reorder_back(values, order):
        return dot_cols(values, order).astype(BF)

    def reorder_wide(values, order):
        top = values.astype(BF)
        return dot(top, order) + dot((values - top.astype(F32)).astype(BF), order)

    qkv_half = 3 * width // 2
    out_half = width // 2
    small = hidden // 4
    planes = [list(range(first, first + 4)) for first in range(0, count, 4)]
    sides = [[i for i in range(count) if (i >> 2) & 1 == side] for side in range(2)]

    def by_side(piece):
        half = piece.shape[-1] // 2
        return take(piece, pair_bit, half, 2), take(piece, 1 - pair_bit, half, 2)

    def line_rows(same, other):
        rows = ordered(pair_bit, jnp.stack(same)[:, None], jnp.stack(other)[:, None], 1)
        return jnp.moveaxis(rows, 2, 0).reshape(2, quarter, -1)

    def line_first(mine, yours):
        same = [mine] + [chip_swap(mine, m << 3) for m in range(1, lines)]
        return same, [chip_swap(yours, (m << 3) | 4) for m in range(lines)]

    def gather_side(mine, got):
        rows = ordered(pair_bit, mine, got, 1)
        rows = jnp.concatenate([rows[0], rows[1]], axis=1)
        return lax.all_gather(rows, "fsdp", axis_index_groups=sides, tiled=True)

    def line_terms(rows, columns):
        return [dot_rows(rows[:, k * quarter : (k + 1) * quarter], columns).astype(BF) for k in range(4)]

    def owner_terms(rows, columns):
        return dot_rows(rows, columns).astype(BF).reshape(4, quarter, -1)

    def line_by_owner(rows):
        parts = [lax.dynamic_slice_in_dim(rows, (k ^ plane) * quarter, quarter, 1) for k in range(4)]
        return jnp.concatenate(parts, axis=1)

    def side_by_owner(rows):
        size = 2 * shard
        parts = [rows[:, (m * 4 + k) * size : (m * 4 + k + 1) * size] for k in range(4) for m in range(lines)]
        return jnp.concatenate(parts, axis=1)

    def plane_sum(terms):
        return lax.psum_scatter(terms, "fsdp", scatter_dimension=0, axis_index_groups=planes)

    def beside(left, right):
        return jnp.concatenate(
            [
                jnp.concatenate([left, jnp.zeros((left.shape[0], right.shape[1]), BF)], axis=1),
                jnp.concatenate([jnp.zeros((right.shape[0], left.shape[1]), BF), right], axis=1),
            ],
            axis=0,
        )

    def line_pieces(totals, relative):
        totals = [total.reshape(lines, 2, shard, -1) for total in totals]

        def pieces(index):
            rows = jnp.concatenate([take(total, index, 1, 1)[:, 0] for total in totals], axis=-1)
            if relative:
                return [rows[m] for m in range(lines)]
            return [lax.dynamic_index_in_dim(rows, (rank >> 3) ^ m, 0, False) for m in range(lines)]

        return pieces(pair_bit), pieces(1 - pair_bit)

    def line_sum_first(pieces):
        mine, yours = pieces
        same = [chip_swap(mine[m], m << 3) for m in range(1, lines)]
        other = [chip_swap(yours[m], (m << 3) | 4) for m in range(lines)]
        return same, other

    def line_sum_whole(pieces, got):
        same, other = got
        mine = pieces[0][0].astype(F32)
        for piece in same:
            mine = mine + piece.astype(F32)
        yours = other[0].astype(F32)
        for piece in other[1:]:
            yours = yours + piece.astype(F32)
        return mine, yours

    def halves(own, other):
        return ordered(core, own, other, 1)

    def gather_tokens(values):
        two = jnp.concatenate([values, chip_swap(values, 4)], axis=0)
        return jnp.concatenate([two, core_swap(two)], axis=0)

    def reduce_tokens(values):
        two = values[: 2 * tokens] + core_swap(values[2 * tokens :].astype(BF)).astype(F32)
        return two[:tokens] + chip_swap(two[tokens:].astype(BF), 4).astype(F32)

    def attn_in(layer, rows_line):
        normed_float, norm_back = jax.vjp(norm_rows, rows_line, *layer_vectors[layer][0])
        return normed_float.astype(BF), norm_back

    def attn_qkv(layer, normed, attn_own, attn_other):
        both = [jnp.concatenate([dot(normed, w) for w in part], axis=1)[:, :qkv_half] for part in (attn_own, attn_other)]
        packed = halves(*both) + layer_vectors[layer][2]
        packed = packed.astype(BF).T
        return jnp.concatenate([to_slots(packed[i * width : (i + 1) * width]) for i in range(3)], axis=1)

    def attn_mix(heads_packed):
        heads_ctx, probs = attend(heads_packed, pack_segments)
        return pack_exchange(heads_ctx), probs

    def attn_out(layer, rows_in, heads_ctx, attn_own, attn_other):
        out_bias, gain, bias, _ = layer_vectors[layer][1]
        context = reorder(from_slots(heads_ctx).T, order_line)
        both = [jnp.concatenate([dot(context, w) for w in part], axis=1)[:, qkv_half:] for part in (attn_own, attn_other)]
        middle = rows_in + reorder_wide(halves(*both), order_side) + out_bias
        normed_float, norm_back = jax.vjp(norm_rows, middle, gain, bias)
        return context, middle, normed_float.astype(BF), norm_back

    def mlp(layer, middle, normed, fc_weight, proj_weight):
        pre_act = dot(normed, fc_weight) + layer_vectors[layer][3]
        activated = gelu_tanh(pre_act).astype(BF)
        result = middle + reduce_tokens(dot_cols(activated, proj_weight)) + layer_vectors[layer][1][3]
        return result, pre_act, activated

    def mlp_back(grad_out_all, pre_act, fc_weight, proj_weight):
        grad_act = dot(grad_out_all, proj_weight)
        grad_pre = jax.vjp(gelu_tanh, pre_act)[1](grad_act)[0].astype(BF)
        return grad_pre, dot_cols(grad_pre, fc_weight)

    def back_through(grad, blocks, first, last):
        total, start = 0.0, 0
        for w in blocks:
            stop = start + w.shape[1]
            low, high = max(first, start), min(last, stop)
            if low < high:
                part = jnp.pad(grad[:, low - first : high - first], ((0, 0), (low - start, stop - high)))
                total += dot_cols(part, w)
            start = stop
        return total

    def attn_out_back(upstream, grad_norm, norm_back, attn_own, attn_other):
        grad_middle_norm, grad_gain, grad_bias = norm_back(grad_norm)
        grad_middle = upstream + grad_middle_norm
        grad_attn_own = grad_middle.astype(BF)
        grad_attn = reorder_back(grad_attn_own, order_side)
        attn_mine, attn_yours = take(grad_attn, core, out_half, 1), take(grad_attn, 1 - core, out_half, 1)
        columns = qkv_half, qkv_half + out_half
        grad_context = back_through(attn_mine, attn_own, *columns) + back_through(attn_yours, attn_other, *columns)
        (grad_context,) = fence(reorder_back(grad_context.astype(BF), order_line))
        heads_grad = pack_exchange(to_slots(grad_context.T))
        return reorder_wide(grad_middle, order_across), grad_attn_own, attn_mine, attn_yours, heads_grad, grad_gain, grad_bias

    def attn_qkv_back(back, grad_middle, norm_back, attn_own, attn_other):
        grad_packed = jnp.concatenate(
            [from_slots(back[:, i * SLOT_COLS : (i + 1) * SLOT_COLS]) for i in range(3)], axis=0
        ).T
        mine, yours = take(grad_packed, core, qkv_half, 1), take(grad_packed, 1 - core, qkv_half, 1)
        grad_normed = back_through(mine, attn_own, 0, qkv_half) + back_through(yours, attn_other, 0, qkv_half)
        grad_rows_norm, grad_gain, grad_bias = norm_back(grad_normed)
        return grad_middle + grad_rows_norm, grad_packed, mine, yours, grad_gain, grad_bias

    def attn_factors(normed, context, qkv_mine, qkv_yours, attn_mine, attn_yours):
        got = core_swap(jnp.concatenate([normed, context, qkv_yours, attn_yours], axis=1))
        normed_both = jnp.concatenate([normed, got[:, :width]], axis=0)
        context_both = jnp.concatenate([context, got[:, width : 2 * width]], axis=0)
        qkv_both = jnp.concatenate([qkv_mine, got[:, 2 * width : 2 * width + qkv_half]], axis=0)
        attn_both = jnp.concatenate([attn_mine, got[:, 2 * width + qkv_half :]], axis=0)
        return normed_both, context_both, qkv_both, attn_both

    def vector_grads(gain_one, bias_one, grad_attn_own, gain_two, bias_two, grad_out_low, grad_packed, grad_pre):
        def natural(rows, order):
            return lax.dot_general(
                jnp.stack(rows),
                order.astype(F32),
                (((1,), (1,)), ((), ())),
                precision=lax.Precision.HIGHEST,
                preferred_element_type=F32,
            )

        out_bias = jnp.sum(grad_attn_own.astype(F32), axis=0)
        proj_bias = jnp.sum(grad_out_low.astype(F32), axis=0)
        model = jnp.concatenate(
            [natural([gain_one, bias_one], order_line), natural([out_bias, gain_two, bias_two, proj_bias], order_side)]
        )
        packed_float = grad_packed.astype(F32)
        qv = jnp.concatenate([jnp.sum(packed_float[:, :width], axis=0), jnp.sum(packed_float[:, 2 * width :], axis=0)])
        fc = lax.dynamic_update_slice_in_dim(
            jnp.zeros((hidden,), F32),
            jnp.sum(grad_pre.astype(F32), axis=0),
            core * (hidden // 2) + pair_bit * small,
            0,
        )
        return jnp.concatenate(
            [model[i].reshape(count, shard) for i in range(6)]
            + [qv.reshape(count, 2 * shard), fc.reshape(count, 4 * shard)],
            axis=1,
        )

    def two(first, second):
        halves_of = []
        for index in (core, 1 - core):
            left, right = [take(p, index, p.shape[1] // 2, 1) for p in (first, second)]
            size = (left.shape[1] + right.shape[1]) // 2
            if left.shape[1] > size:
                left, right = left[:, :size], jnp.concatenate([left[:, size:], right], axis=1)
            halves_of.append(jnp.stack([left, right]))
        mine, yours = halves_of
        got = core_swap(yours)
        return [jnp.where(core == layer, mine, got) for layer in range(2)]

    attn_shards = two(w_qkv[0], w_out[0])
    vectors = jnp.concatenate(
        [
            ln1_gain[0],
            ln1_bias[0],
            b_out[0],
            ln2_gain[0],
            ln2_bias[0],
            b_proj[0],
            b_qv[0],
            b_fc[0],
            lax.dynamic_index_in_dim(segments, core, 0, False).astype(BF),
        ]
    )
    (a0, a1), vectors = fence(attn_shards, vectors)

    a0_line = line_first(a0, a0)
    mlp_shards = two(w_fc[0], w_proj[0])
    m0, m0_yours = by_side(mlp_shards[0])
    m1, m1_yours = by_side(mlp_shards[1])
    vector_rows = vectors[None]
    for bit in range(bits):
        vector_rows = gather_bit(vector_rows, bit)
    a0_line, a1, m0, m0_yours, m1, m1_yours, vector_rows = fence(
        a0_line, a1, m0, m0_yours, m1, m1_yours, vector_rows
    )

    a0_quarter = line_rows(*a0_line)
    a0_got = plane_first(a0_quarter)
    a1_line = line_first(a1, a1)
    m0_near = chip_swap(m0_yours, 4)
    own_inputs = lax.dynamic_index_in_dim(inputs, core, 0, False)
    own_cotangent = lax.dynamic_index_in_dim(cotangent, core, 0, False)
    order_line = (place[:, None] == natural_line[None, :]).astype(BF)
    order_side = (place[:, None] == natural_side[None, :]).astype(BF)
    order_across = (natural_side[:, None] == natural_line[None, :]).astype(BF)
    a0_quarter, a0_got, a1_line, m0_near, order_line, order_side, order_across, vector_rows, own_cotangent = fence(
        a0_quarter, a0_got, a1_line, m0_near, order_line, order_side, order_across, vector_rows, own_cotangent
    )

    a0_across = plane_second(a0_got)
    a0_quarter_other, a0_got_other = core_swap(a0_quarter), (core_swap(a0_got[0]), core_swap(a0_got[1]))
    a1_quarter = line_rows(*a1_line)
    a1_got = plane_first(a1_quarter)
    segment_rows = vector_rows[:, 12 * shard :].astype(jnp.int32)
    pack_segments = take(segment_rows, rank // PACK_DEVS, PACK_DEVS, 0).reshape(-1)
    vector_rows = vector_rows[:, : 12 * shard]
    vector_other = core_swap(vector_rows)
    layer_vectors = []
    for layer in range(2):
        rows = jnp.where(core == layer, vector_rows, vector_other)
        model = jnp.stack([rows[:, i * shard : (i + 1) * shard].reshape(width) for i in range(6)])
        norm_one, rest = dot(model[:2], order_line), dot(model[2:], order_side)
        qv = rows[:, 6 * shard : 8 * shard].reshape(2 * width).astype(F32)
        fc = rows[:, 8 * shard : 12 * shard].reshape(hidden).astype(F32)
        fc = lax.dynamic_slice_in_dim(fc, core * (hidden // 2) + pair_bit * (hidden // 4), hidden // 4, 0)
        qkv = jnp.concatenate([qv[:width], jnp.zeros((width,), F32), qv[width:]])
        layer_vectors.append(((norm_one[0], norm_one[1]), (rest[0], rest[1], rest[2], rest[3]), qkv, fc))
    first_in = reorder(own_inputs, order_side).astype(F32)
    first_line = reorder(own_inputs, order_line).astype(F32)
    first_normed, first_norm_one = attn_in(0, first_line)
    second_up_low = reorder(own_cotangent, order_side)
    second_up_all = gather_tokens(second_up_low)
    (
        a0_across,
        a0_quarter_other,
        a0_got_other,
        a1_quarter,
        a1_got,
        first_normed,
        second_up_low,
        second_up_all,
        m0,
        m0_near,
        m1_yours,
    ) = fence(
        a0_across,
        a0_quarter_other,
        a0_got_other,
        a1_quarter,
        a1_got,
        first_normed,
        second_up_low,
        second_up_all,
        m0,
        m0_near,
        m1_yours,
    )

    mlp_first = gather_side(m0, m0_near)
    a1_across = plane_second(a1_got)
    a0_across_other = [core_swap(part) for part in a0_across]
    attn_first = (
        plane_whole(a0_quarter, a0_got, a0_across),
        plane_whole(a0_quarter_other, a0_got_other, a0_across_other),
    )
    sent = attn_qkv(0, first_normed, *attn_first)
    sent, a1_across, m1_yours = fence(sent, a1_across, m1_yours)

    m1_near = chip_swap(m1_yours, 4)
    first_heads = pack_exchange(sent)
    first_ctx, first_probs = attn_mix(first_heads)
    attn_second = plane_whole(a1_quarter, a1_got, a1_across)
    attn_second = attn_second, tuple(core_swap(part) for part in attn_second)
    first_context, first_middle, first_normed_two, first_norm_two = attn_out(0, first_in, first_ctx, *attn_first)
    first_normed_two, mlp_first, m1, m1_near = fence(first_normed_two, mlp_first, m1, m1_near)
    mlp_second = gather_side(m1, m1_near)
    first_normed_two = gather_tokens(first_normed_two)
    mlp_first = mlp_first[:, :small], mlp_first[:, small:]
    first_out, first_pre, first_act = mlp(0, first_middle, first_normed_two, *mlp_first)
    first_low = first_out.astype(BF)
    second_in = first_low.astype(F32)
    second_line = reorder(first_low, order_across).astype(F32)
    second_normed, second_norm_one = attn_in(1, second_line)
    second_heads = pack_exchange(attn_qkv(1, second_normed, *attn_second))
    second_ctx, second_probs = attn_mix(second_heads)
    second_ctx, mlp_second = fence(second_ctx, mlp_second)
    second_context, second_middle, second_normed_two, second_norm_two = attn_out(1, second_in, second_ctx, *attn_second)
    second_normed_two = gather_tokens(second_normed_two)
    mlp_second = mlp_second[:, :small], mlp_second[:, small:]
    second_out, second_pre, second_act = mlp(1, second_middle, second_normed_two, *mlp_second)
    second_low = second_out.astype(BF)

    second_up = second_up_low.astype(F32)
    second_pre_grad, part = mlp_back(second_up_all, second_pre, *mlp_second)
    second_pre_grad, part = fence(second_pre_grad, part)
    grad_norm = reduce_tokens(part)
    f1_terms = owner_terms(side_by_owner(second_normed_two), second_pre_grad)
    p1_terms = owner_terms(side_by_owner(second_up_all), second_act)
    grad_norm, f1_terms, p1_terms = fence(grad_norm, f1_terms, p1_terms)
    f1_sum, p1_sum = plane_sum(f1_terms), plane_sum(p1_terms)
    second_mid_grad, second_da, attn_mine, attn_yours, heads_grad, second_gain_two, second_bias_two = attn_out_back(
        second_up, grad_norm, second_norm_two, *attn_second
    )
    back = pack_exchange(attend_back(second_heads, second_probs, heads_grad))
    second_grad, second_packed, qkv_mine, qkv_yours, second_gain_one, second_bias_one = attn_qkv_back(
        back, second_mid_grad, second_norm_one, *attn_second
    )
    second_grad_low = second_grad.astype(BF)
    first_up_low = reorder_back(second_grad_low, order_across)
    first_up_low, qkv_mine, qkv_yours = fence(first_up_low, qkv_mine, qkv_yours)
    first_up = first_up_low.astype(F32)
    first_up_all = gather_tokens(first_up_low)
    normed_both, context_both, qkv_both, attn_both = attn_factors(
        second_normed, second_context, qkv_mine, qkv_yours, attn_mine, attn_yours
    )
    q1_terms = owner_terms(line_by_owner(normed_both), qkv_both)
    o1_terms = owner_terms(line_by_owner(context_both), attn_both)
    first_up_all, q1_terms, o1_terms, f1_sum = fence(first_up_all, q1_terms, o1_terms, f1_sum)
    q1_sum, o1_sum = plane_sum(q1_terms), plane_sum(o1_terms)
    first_pre_grad, part = mlp_back(first_up_all, first_pre, *mlp_first)
    first_pre_grad, part = fence(first_pre_grad, part)
    grad_norm = reduce_tokens(part)
    f0_terms = owner_terms(side_by_owner(first_normed_two), first_pre_grad)
    p0_terms = owner_terms(side_by_owner(first_up_all), first_act)
    grad_norm, f0_terms, p0_terms, p1_sum = fence(grad_norm, f0_terms, p0_terms, p1_sum)
    f0_sum, p0_sum = plane_sum(f0_terms), plane_sum(p0_terms)
    m1_pieces = line_pieces((f1_sum, p1_sum), False)
    m1_got = line_sum_first(m1_pieces)
    first_mid_grad, first_da, attn_mine, attn_yours, heads_grad, first_gain_two, first_bias_two = attn_out_back(
        first_up, grad_norm, first_norm_two, *attn_first
    )
    heads_grad, first_mid_grad, m1_got, attn_mine, attn_yours, q1_sum = fence(
        heads_grad, first_mid_grad, m1_got, attn_mine, attn_yours, q1_sum
    )
    def by_section(first, second):
        own = jnp.where(core == 0, first, second)
        got = core_swap(jnp.where(core == 0, second, first))
        return ordered(core, own[None], got[None], 0)

    back = pack_exchange(attend_back(first_heads, first_probs, heads_grad))
    section_outputs = by_section(reorder_back(first_low, order_side), reorder_back(second_low, order_side))
    second_vectors = vector_grads(
        second_gain_one,
        second_bias_one,
        second_da,
        second_gain_two,
        second_bias_two,
        second_up_low,
        second_packed,
        second_pre_grad,
    )
    back, o1_sum, section_outputs, second_vectors = fence(back, o1_sum, section_outputs, second_vectors)
    a1_pieces = line_pieces((q1_sum, o1_sum), True)
    a1_got = line_sum_first(a1_pieces)
    first_grad, first_packed, qkv_mine, qkv_yours, first_gain_one, first_bias_one = attn_qkv_back(
        back, first_mid_grad, first_norm_one, *attn_first
    )
    first_grad_low = first_grad.astype(BF)
    normed_both, context_both, qkv_both, attn_both = attn_factors(
        first_normed, first_context, qkv_mine, qkv_yours, attn_mine, attn_yours
    )
    a0_left = line_terms(normed_both, qkv_both[:, :width])
    a0_right = line_terms(
        jnp.concatenate([normed_both, context_both], axis=0), beside(qkv_both[:, width:], attn_both)
    )
    a0_left, a0_right, first_grad_low = fence(a0_left, a0_right, first_grad_low)
    a0_got = sum_first(a0_left, a0_right)
    a0_got, a1_got, f0_sum, p0_sum, first_grad_low, first_packed = fence(
        a0_got, a1_got, f0_sum, p0_sum, first_grad_low, first_packed
    )
    first_vectors = vector_grads(
        first_gain_one,
        first_bias_one,
        first_da,
        first_gain_two,
        first_bias_two,
        first_up_low,
        first_packed,
        first_pre_grad,
    )
    vector_rows = jnp.where(core == 0, first_vectors, second_vectors) + core_swap(
        jnp.where(core == 0, second_vectors, first_vectors)
    )
    a0_last = sum_second(a0_left, a0_right, a0_got)
    m0_pieces = line_pieces((f0_sum, p0_sum), False)
    m0_got = line_sum_first(m0_pieces)
    input_grads = by_section(
        reorder_back(first_grad_low, order_line), reorder_back(second_grad_low, order_line)
    )
    a0_last, m0_got, input_grads, vector_rows = fence(a0_last, m0_got, input_grads, vector_rows)
    vector_own = reduce_vector(vector_rows)
    a0_pieces = line_pieces(sum_whole(a0_left, a0_right, a0_got, a0_last), True)
    a0_got = line_sum_first(a0_pieces)

    def matrix_grads(attn_pieces, attn_got, mlp_pieces, mlp_got):
        same, other = line_sum_whole(attn_pieces, attn_got)
        attn = same + other
        same, other = line_sum_whole(mlp_pieces, mlp_got)
        return (
            attn[:, :qkv_half],
            attn[:, qkv_half:],
            ordered(pair_bit, same[:, :small], other[:, :small], 1),
            ordered(pair_bit, same[:, small:], other[:, small:], 1),
        )

    first_mats = matrix_grads(a0_pieces, a0_got, m0_pieces, m0_got)
    second_mats = matrix_grads(a1_pieces, a1_got, m1_pieces, m1_got)
    mats = []
    for first, second in zip(first_mats, second_mats):
        own = jnp.where(core == 0, first, second)
        got = core_swap(jnp.where(core == 0, second, first))
        mats.append(ordered(core, own, got, 1))
    model = [vector_own[i * shard : (i + 1) * shard] for i in range(6)]
    return (
        section_outputs[None],
        input_grads[None],
        model[0][None],
        model[1][None],
        mats[0][None],
        vector_own[6 * shard : 8 * shard][None],
        mats[1][None],
        model[2][None],
        model[3][None],
        model[4][None],
        mats[2][None],
        vector_own[8 * shard :][None],
        mats[3][None],
        model[5][None],
    )


def solution(mesh):
    in_specs = (
        P(None, "fsdp", None),
        P(None, "fsdp", None),
        P(None, "fsdp"),
        P("section", "fsdp"),
        P("section", "fsdp"),
        P("section", "fsdp", None),
        P("section", "fsdp"),
        P("section", "fsdp", None),
        P("section", "fsdp"),
        P("section", "fsdp"),
        P("section", "fsdp"),
        P("section", "fsdp", None),
        P("section", "fsdp"),
        P("section", "fsdp", None),
        P("section", "fsdp"),
    )
    out_specs = (
        P("section", None, "fsdp", None),
        P("section", None, "fsdp", None),
        P("section", "fsdp"),
        P("section", "fsdp"),
        P("section", "fsdp", None),
        P("section", "fsdp"),
        P("section", "fsdp", None),
        P("section", "fsdp"),
        P("section", "fsdp"),
        P("section", "fsdp"),
        P("section", "fsdp", None),
        P("section", "fsdp"),
        P("section", "fsdp", None),
        P("section", "fsdp"),
    )
    return jax.shard_map(
        on_device, mesh=mesh, in_specs=in_specs, out_specs=out_specs, check_vma=False
    )
```

```python
import math

import jax
import jax.numpy as jnp
from jax import lax
from jax.experimental import pallas as pl
from jax.experimental.pallas import tpu as pltpu
from jax.sharding import PartitionSpec as P

HEADS = 25
HEAD_DIM = 64
SEQ_LEN = 1024
PACK_DEVS = 8
MAIN = HEADS // PACK_DEVS
SLOTS = 4
SLOT_COLS = SLOTS * HEAD_DIM
BLOCK = 256
BF = jnp.bfloat16
F32 = jnp.float32


def chip_swap(value, mask):
    count = lax.axis_size("fsdp")
    return lax.ppermute(value, "fsdp", [(i, i ^ mask) for i in range(count)])


def core_swap(value):
    return lax.ppermute(value, "section", [(0, 1), (1, 0)])


def fence(*values):
    return lax.optimization_barrier(values)


def ordered(bit, own, other, axis):
    return jnp.where(
        bit == 0,
        jnp.concatenate([own, other], axis=axis),
        jnp.concatenate([other, own], axis=axis),
    )


def take(value, index, size, axis):
    return lax.dynamic_slice_in_dim(value, index * size, size, axis)


def dot(left, right):
    return jnp.dot(left, right, preferred_element_type=F32)


def dot_rows(left, right):
    return lax.dot_general(left, right, (((0,), (0,)), ((), ())), preferred_element_type=F32)


def dot_cols(left, right):
    return lax.dot_general(left, right, (((1,), (1,)), ((), ())), preferred_element_type=F32)


def norm_rows(values, gain_vec, bias_vec):
    row_mean = jnp.mean(values, axis=-1, keepdims=True)
    centered = values - row_mean
    variance = jnp.mean(centered * centered, axis=-1, keepdims=True)
    return centered * lax.rsqrt(variance + 1e-05) * gain_vec + bias_vec


def gelu_tanh(values):
    return jax.nn.gelu(values, approximate=True)


def tokens_of(ref, first_row, blocks):
    rows = slice(first_row, first_row + HEAD_DIM)
    return jnp.concatenate([ref[s, rows, :] for s in range(blocks)], axis=1)


def attend_kernel(q_ref, k_ref, v_ref, srow_ref, scol_ref, ctx_ref, p_ref, bias_ref):
    per = q_ref.shape[2]
    length = q_ref.shape[0] * per
    step = BLOCK // per

    @pl.when(pl.program_id(0) == 0)
    def _():
        for first in range(0, length, BLOCK):
            wide = first + BLOCK
            key = lax.broadcasted_iota(jnp.int32, (wide, BLOCK), 0)
            query = lax.broadcasted_iota(jnp.int32, (wide, BLOCK), 1) + first
            same = scol_ref[:wide, :] == srow_ref[:, first:wide]
            bias_ref[:wide, first:wide] = jnp.where(same & (key <= query), 0.0, -1e30)

    for h in range(2):
        row = h * HEAD_DIM
        keys = tokens_of(k_ref, row, length // per)
        values = tokens_of(v_ref, row, length // per)
        queries = tokens_of(q_ref, row, length // per) * jnp.asarray(1.0 / math.sqrt(HEAD_DIM), BF)
        for first in range(0, length, BLOCK):
            wide = first + BLOCK
            s = dot_rows(keys[:, :wide], queries[:, first:wide]) + bias_ref[:wide, first:wide]
            m = jnp.max(s, axis=0, keepdims=True)
            e = jnp.exp(s - m)
            p = (e * (1.0 / jnp.sum(e, axis=0, keepdims=True))).astype(BF)
            p_ref[h, :wide, first:wide] = p
            ctx = dot(values[:, :wide], p).astype(BF)
            for i in range(step):
                ctx_ref[first // per + i, row : row + HEAD_DIM, :] = ctx[:, i * per : (i + 1) * per]


def attend_back_kernel(q_ref, k_ref, v_ref, p_ref, d_ref, back_ref, dk_sum, dv_sum):
    per = q_ref.shape[2]
    length = q_ref.shape[0] * per
    step = BLOCK // per
    scale = jnp.asarray(1.0 / math.sqrt(HEAD_DIM), BF)
    for h in range(2):
        row = h * HEAD_DIM
        rows = slice(row, row + HEAD_DIM)
        keys = tokens_of(k_ref, row, length // per) * scale
        values = tokens_of(v_ref, row, length // per)
        queries = tokens_of(q_ref, row, length // per) * scale
        grads = tokens_of(d_ref, row, length // per)
        for first in reversed(range(0, length, BLOCK)):
            wide = first + BLOCK
            d = grads[:, first:wide]
            p_low = p_ref[h, :wide, first:wide]
            dp = dot_rows(values[:, :wide], d)
            p = p_low.astype(F32)
            ds = (p * (dp - jnp.sum(p * dp, axis=0, keepdims=True))).astype(BF)
            dq = dot(keys[:, :wide], ds).astype(BF)
            for i in range(step):
                back_ref[first // per + i, 0, rows, :] = dq[:, i * per : (i + 1) * per]
            dk = dot_cols(queries[:, first:wide], ds)
            dv = dot_cols(d, p_low)
            if wide == length:
                dk_sum[...] = dk
                dv_sum[...] = dv
            else:
                dk_sum[:, :wide] += dk
                dv_sum[:, :wide] += dv
        for s in range(length // per):
            back_ref[s, 1, rows, :] = dk_sum[:, s * per : (s + 1) * per].astype(BF)
            back_ref[s, 2, rows, :] = dv_sum[:, s * per : (s + 1) * per].astype(BF)


def attend(packed, segs):
    devices, _, per = packed.shape
    length = devices * per
    pairs = SLOTS // 2
    rows = 2 * HEAD_DIM
    return pl.pallas_call(
        attend_kernel,
        grid=(pairs,),
        in_specs=[
            pl.BlockSpec((devices, rows, per), lambda g: (0, g, 0)),
            pl.BlockSpec((devices, rows, per), lambda g: (0, pairs + g, 0)),
            pl.BlockSpec((devices, rows, per), lambda g: (0, 2 * pairs + g, 0)),
            pl.BlockSpec((1, length), lambda g: (0, 0)),
            pl.BlockSpec((length, 1), lambda g: (0, 0)),
        ],
        out_specs=[
            pl.BlockSpec((devices, rows, per), lambda g: (0, g, 0)),
            pl.BlockSpec((2, length, length), lambda g: (g, 0, 0)),
        ],
        out_shape=[
            jax.ShapeDtypeStruct((devices, SLOT_COLS, per), BF),
            jax.ShapeDtypeStruct((SLOTS, length, length), BF),
        ],
        scratch_shapes=[pltpu.VMEM((length, length), F32)],
        compiler_params=pltpu.CompilerParams(vmem_limit_bytes=48 * 1024 * 1024),
        cost_estimate=pl.CostEstimate(flops=12 * 10**9, bytes_accessed=12 * 10**6, transcendentals=0),
    )(packed, packed, packed, segs.reshape(1, length), segs.reshape(length, 1))


def attend_back(packed, probs, grad):
    devices, _, per = packed.shape
    length = devices * per
    pairs = SLOTS // 2
    rows = 2 * HEAD_DIM
    pair_block = pl.BlockSpec((devices, rows, per), lambda g: (0, g, 0))
    back = pl.pallas_call(
        attend_back_kernel,
        grid=(pairs,),
        in_specs=[
            pair_block,
            pl.BlockSpec((devices, rows, per), lambda g: (0, pairs + g, 0)),
            pl.BlockSpec((devices, rows, per), lambda g: (0, 2 * pairs + g, 0)),
            pl.BlockSpec((2, length, length), lambda g: (g, 0, 0)),
            pair_block,
        ],
        out_specs=pl.BlockSpec((devices, 3, rows, per), lambda g: (0, 0, g, 0)),
        out_shape=jax.ShapeDtypeStruct((devices, 3, SLOT_COLS, per), BF),
        scratch_shapes=[pltpu.VMEM((HEAD_DIM, length), F32)] * 2,
        compiler_params=pltpu.CompilerParams(vmem_limit_bytes=48 * 1024 * 1024),
        cost_estimate=pl.CostEstimate(flops=24 * 10**9, bytes_accessed=12 * 10**6, transcendentals=0),
    )(packed, packed, packed, probs, grad)
    return back.reshape(devices, 3 * SLOT_COLS, per)


def to_slots(values):
    split = PACK_DEVS * MAIN * HEAD_DIM
    main = values[:split].reshape(PACK_DEVS, MAIN * HEAD_DIM, -1)
    last = values[None, split:]
    none = jnp.zeros((PACK_DEVS - 1,) + last.shape[1:], values.dtype)
    return jnp.concatenate([main, jnp.concatenate([last, none], axis=0)], axis=1)


def from_slots(slots):
    main = slots[:, : MAIN * HEAD_DIM].reshape(PACK_DEVS * MAIN * HEAD_DIM, -1)
    return jnp.concatenate([main, slots[0, MAIN * HEAD_DIM :]], axis=0)


def pack_exchange(value):
    count = lax.axis_size("fsdp")
    groups = [list(range(first, first + PACK_DEVS)) for first in range(0, count, PACK_DEVS)]
    return lax.all_to_all(value, "fsdp", 0, 0, axis_index_groups=groups)


def plane_first(quarter):
    return chip_swap(quarter, 1), chip_swap(quarter, 2)


def plane_second(got):
    return chip_swap(got[0][0], 2), chip_swap(got[1][1], 1)


def plane_whole(quarter, got, across):
    return tuple(jnp.concatenate([quarter[i], got[0][i], got[1][i], across[i]], axis=0) for i in range(2))


def sum_first(left, right):
    return chip_swap(left[3], 2), chip_swap(right[3], 1)


def sum_second(left, right, got):
    to_x = jnp.stack([(left[1].astype(F32) + got[0].astype(F32)).astype(BF), right[1]])
    to_y = jnp.stack([left[2], (right[2].astype(F32) + got[1].astype(F32)).astype(BF)])
    return chip_swap(to_x, 1), chip_swap(to_y, 2)


def sum_whole(left, right, last):
    from_x, from_y = last
    return [
        (own.astype(F32) + from_x[i].astype(F32) + from_y[i].astype(F32)).astype(BF)
        for i, own in enumerate((left[0], right[0]))
    ]


def bits_of(count):
    return count.bit_length() - 1


def gather_bit(rows, bit):
    return ordered((lax.axis_index("fsdp") >> bit) & 1, rows, chip_swap(rows, 1 << bit), 0)


def reduce_vector(rows):
    index = lax.axis_index("fsdp")
    for bit in range(bits_of(lax.axis_size("fsdp"))):
        split = rows.reshape(-1, 2, rows.shape[-1])
        mine = (index >> bit) & 1
        rows = take(split, mine, 1, 1) + chip_swap(take(split, 1 - mine, 1, 1), 1 << bit)
        rows = rows[:, 0]
    return rows[0]


def on_device(
    inputs,
    cotangent,
    segments,
    ln1_gain,
    ln1_bias,
    w_qkv,
    b_qv,
    w_out,
    b_out,
    ln2_gain,
    ln2_bias,
    w_fc,
    b_fc,
    w_proj,
    b_proj,
):
    core = lax.axis_index("section")
    rank = lax.axis_index("fsdp")
    count = lax.axis_size("fsdp")
    bits = bits_of(count)
    tokens, width = inputs.shape[1:]
    shard = w_qkv.shape[1]
    hidden = w_fc.shape[2]
    quarter = width // 4
    pair_bit = (rank >> 2) & 1
    plane = rank & 3

    lines = count // 8

    place = jnp.arange(width, dtype=jnp.int32)
    block = place // shard
    line = block % (2 * lines)
    natural_line = ((((rank >> 3) ^ (line >> 1)) << 1) | (line & 1)) * 4 + ((place // quarter) ^ plane)
    natural_line = natural_line * shard + place % shard
    natural_side = (((block >> 3) * 2 + (block & 1)) * 4 + ((block >> 1) & 3)) * shard + place % shard

    def reorder(values, order):
        return dot(values, order).astype(BF)

    def reorder_back(values, order):
        return dot_cols(values, order).astype(BF)

    def reorder_wide(values, order):
        top = values.astype(BF)
        return dot(top, order) + dot((values - top.astype(F32)).astype(BF), order)

    qkv_half = 3 * width // 2
    out_half = width // 2
    small = hidden // 4
    planes = [list(range(first, first + 4)) for first in range(0, count, 4)]
    sides = [[i for i in range(count) if (i >> 2) & 1 == side] for side in range(2)]

    def by_side(piece):
        half = piece.shape[-1] // 2
        return take(piece, pair_bit, half, 2), take(piece, 1 - pair_bit, half, 2)

    def line_rows(same, other):
        rows = ordered(pair_bit, jnp.stack(same)[:, None], jnp.stack(other)[:, None], 1)
        return jnp.moveaxis(rows, 2, 0).reshape(2, quarter, -1)

    def line_first(mine, yours):
        same = [mine] + [chip_swap(mine, m << 3) for m in range(1, lines)]
        return same, [chip_swap(yours, (m << 3) | 4) for m in range(lines)]

    def gather_side(mine, got):
        rows = ordered(pair_bit, mine, got, 1)
        rows = jnp.concatenate([rows[0], rows[1]], axis=1)
        return lax.all_gather(rows, "fsdp", axis_index_groups=sides, tiled=True)

    def line_terms(rows, columns):
        return [dot_rows(rows[:, k * quarter : (k + 1) * quarter], columns).astype(BF) for k in range(4)]

    def owner_terms(rows, columns):
        return dot_rows(rows, columns).astype(BF).reshape(4, quarter, -1)

    def line_by_owner(rows):
        parts = [lax.dynamic_slice_in_dim(rows, (k ^ plane) * quarter, quarter, 1) for k in range(4)]
        return jnp.concatenate(parts, axis=1)

    def side_by_owner(rows):
        size = 2 * shard
        parts = [rows[:, (m * 4 + k) * size : (m * 4 + k + 1) * size] for k in range(4) for m in range(lines)]
        return jnp.concatenate(parts, axis=1)

    def plane_sum(terms):
        return lax.psum_scatter(terms, "fsdp", scatter_dimension=0, axis_index_groups=planes)

    def beside(left, right):
        return jnp.concatenate(
            [
                jnp.concatenate([left, jnp.zeros((left.shape[0], right.shape[1]), BF)], axis=1),
                jnp.concatenate([jnp.zeros((right.shape[0], left.shape[1]), BF), right], axis=1),
            ],
            axis=0,
        )

    def line_pieces(totals, relative):
        totals = [total.reshape(lines, 2, shard, -1) for total in totals]

        def pieces(index):
            rows = jnp.concatenate([take(total, index, 1, 1)[:, 0] for total in totals], axis=-1)
            if relative:
                return [rows[m] for m in range(lines)]
            return [lax.dynamic_index_in_dim(rows, (rank >> 3) ^ m, 0, False) for m in range(lines)]

        return pieces(pair_bit), pieces(1 - pair_bit)

    def line_sum_first(pieces):
        mine, yours = pieces
        same = [chip_swap(mine[m], m << 3) for m in range(1, lines)]
        other = [chip_swap(yours[m], (m << 3) | 4) for m in range(lines)]
        return same, other

    def line_sum_whole(pieces, got):
        same, other = got
        mine = pieces[0][0].astype(F32)
        for piece in same:
            mine = mine + piece.astype(F32)
        yours = other[0].astype(F32)
        for piece in other[1:]:
            yours = yours + piece.astype(F32)
        return mine, yours

    def halves(own, other):
        return ordered(core, own, other, 1)

    def gather_tokens(values):
        two = jnp.concatenate([values, chip_swap(values, 4)], axis=0)
        return jnp.concatenate([two, core_swap(two)], axis=0)

    def reduce_tokens(values):
        two = values[: 2 * tokens] + core_swap(values[2 * tokens :].astype(BF)).astype(F32)
        return two[:tokens] + chip_swap(two[tokens:].astype(BF), 4).astype(F32)

    def attn_in(layer, rows_line):
        normed_float, norm_back = jax.vjp(norm_rows, rows_line, *layer_vectors[layer][0])
        return normed_float.astype(BF), norm_back

    def attn_qkv(layer, normed, attn_own, attn_other):
        both = [jnp.concatenate([dot(normed, w) for w in part], axis=1)[:, :qkv_half] for part in (attn_own, attn_other)]
        packed = halves(*both) + layer_vectors[layer][2]
        packed = packed.astype(BF).T
        return jnp.concatenate([to_slots(packed[i * width : (i + 1) * width]) for i in range(3)], axis=1)

    def attn_mix(heads_packed):
        heads_ctx, probs = attend(heads_packed, pack_segments)
        return pack_exchange(heads_ctx), probs

    def attn_out(layer, rows_in, heads_ctx, attn_own, attn_other):
        out_bias, gain, bias, _ = layer_vectors[layer][1]
        context = reorder(from_slots(heads_ctx).T, order_line)
        both = [jnp.concatenate([dot(context, w) for w in part], axis=1)[:, qkv_half:] for part in (attn_own, attn_other)]
        middle = rows_in + reorder_wide(halves(*both), order_side) + out_bias
        normed_float, norm_back = jax.vjp(norm_rows, middle, gain, bias)
        return context, middle, normed_float.astype(BF), norm_back

    def mlp(layer, middle, normed, fc_weight, proj_weight):
        pre_act = dot(normed, fc_weight) + layer_vectors[layer][3]
        activated = gelu_tanh(pre_act).astype(BF)
        result = middle + reduce_tokens(dot_cols(activated, proj_weight)) + layer_vectors[layer][1][3]
        return result, pre_act, activated

    def mlp_back(grad_out_all, pre_act, fc_weight, proj_weight):
        grad_act = dot(grad_out_all, proj_weight)
        grad_pre = jax.vjp(gelu_tanh, pre_act)[1](grad_act)[0].astype(BF)
        return grad_pre, dot_cols(grad_pre, fc_weight)

    def back_through(grad, blocks, first, last):
        total, start = 0.0, 0
        for w in blocks:
            stop = start + w.shape[1]
            low, high = max(first, start), min(last, stop)
            if low < high:
                part = jnp.pad(grad[:, low - first : high - first], ((0, 0), (low - start, stop - high)))
                total += dot_cols(part, w)
            start = stop
        return total

    def attn_out_back(upstream, grad_norm, norm_back, attn_own, attn_other):
        grad_middle_norm, grad_gain, grad_bias = norm_back(grad_norm)
        grad_middle = upstream + grad_middle_norm
        grad_attn_own = grad_middle.astype(BF)
        grad_attn = reorder_back(grad_attn_own, order_side)
        attn_mine, attn_yours = take(grad_attn, core, out_half, 1), take(grad_attn, 1 - core, out_half, 1)
        columns = qkv_half, qkv_half + out_half
        grad_context = back_through(attn_mine, attn_own, *columns) + back_through(attn_yours, attn_other, *columns)
        (grad_context,) = fence(reorder_back(grad_context.astype(BF), order_line))
        heads_grad = pack_exchange(to_slots(grad_context.T))
        return reorder_wide(grad_middle, order_across), grad_attn_own, attn_mine, attn_yours, heads_grad, grad_gain, grad_bias

    def attn_qkv_back(back, grad_middle, norm_back, attn_own, attn_other):
        grad_packed = jnp.concatenate(
            [from_slots(back[:, i * SLOT_COLS : (i + 1) * SLOT_COLS]) for i in range(3)], axis=0
        ).T
        mine, yours = take(grad_packed, core, qkv_half, 1), take(grad_packed, 1 - core, qkv_half, 1)
        grad_normed = back_through(mine, attn_own, 0, qkv_half) + back_through(yours, attn_other, 0, qkv_half)
        grad_rows_norm, grad_gain, grad_bias = norm_back(grad_normed)
        return grad_middle + grad_rows_norm, grad_packed, mine, yours, grad_gain, grad_bias

    def attn_factors(normed, context, qkv_mine, qkv_yours, attn_mine, attn_yours):
        got = core_swap(jnp.concatenate([normed, context, qkv_yours, attn_yours], axis=1))
        normed_both = jnp.concatenate([normed, got[:, :width]], axis=0)
        context_both = jnp.concatenate([context, got[:, width : 2 * width]], axis=0)
        qkv_both = jnp.concatenate([qkv_mine, got[:, 2 * width : 2 * width + qkv_half]], axis=0)
        attn_both = jnp.concatenate([attn_mine, got[:, 2 * width + qkv_half :]], axis=0)
        return normed_both, context_both, qkv_both, attn_both

    def vector_grads(gain_one, bias_one, grad_attn_own, gain_two, bias_two, grad_out_low, grad_packed, grad_pre):
        def natural(rows, order):
            return lax.dot_general(
                jnp.stack(rows),
                order.astype(F32),
                (((1,), (1,)), ((), ())),
                precision=lax.Precision.HIGHEST,
                preferred_element_type=F32,
            )

        out_bias = jnp.sum(grad_attn_own.astype(F32), axis=0)
        proj_bias = jnp.sum(grad_out_low.astype(F32), axis=0)
        model = jnp.concatenate(
            [natural([gain_one, bias_one], order_line), natural([out_bias, gain_two, bias_two, proj_bias], order_side)]
        )
        packed_float = grad_packed.astype(F32)
        qv = jnp.concatenate([jnp.sum(packed_float[:, :width], axis=0), jnp.sum(packed_float[:, 2 * width :], axis=0)])
        fc = lax.dynamic_update_slice_in_dim(
            jnp.zeros((hidden,), F32),
            jnp.sum(grad_pre.astype(F32), axis=0),
            core * (hidden // 2) + pair_bit * small,
            0,
        )
        return jnp.concatenate(
            [model[i].reshape(count, shard) for i in range(6)]
            + [qv.reshape(count, 2 * shard), fc.reshape(count, 4 * shard)],
            axis=1,
        )

    def two(first, second):
        halves_of = []
        for index in (core, 1 - core):
            left, right = [take(p, index, p.shape[1] // 2, 1) for p in (first, second)]
            size = (left.shape[1] + right.shape[1]) // 2
            if left.shape[1] > size:
                left, right = left[:, :size], jnp.concatenate([left[:, size:], right], axis=1)
            halves_of.append(jnp.stack([left, right]))
        mine, yours = halves_of
        got = core_swap(yours)
        return [jnp.where(core == layer, mine, got) for layer in range(2)]

    attn_shards = two(w_qkv[0], w_out[0])
    vectors = jnp.concatenate(
        [
            ln1_gain[0],
            ln1_bias[0],
            b_out[0],
            ln2_gain[0],
            ln2_bias[0],
            b_proj[0],
            b_qv[0],
            b_fc[0],
            lax.dynamic_index_in_dim(segments, core, 0, False).astype(BF),
        ]
    )
    (a0, a1), vectors = fence(attn_shards, vectors)

    a0_line = line_first(a0, a0)
    mlp_shards = two(w_fc[0], w_proj[0])
    m0, m0_yours = by_side(mlp_shards[0])
    m1, m1_yours = by_side(mlp_shards[1])
    a0_line, a1, m0, m0_yours, m1, m1_yours, vectors = fence(a0_line, a1, m0, m0_yours, m1, m1_yours, vectors)

    a0_quarter = line_rows(*a0_line)
    a0_got = plane_first(a0_quarter)
    a1_line = line_first(a1, a1)
    m0_near = chip_swap(m0_yours, 4)
    vector_rows = vectors[None]
    for bit in range(bits):
        vector_rows = gather_bit(vector_rows, bit)
    own_inputs = lax.dynamic_index_in_dim(inputs, core, 0, False)
    own_cotangent = lax.dynamic_index_in_dim(cotangent, core, 0, False)
    order_line = (place[:, None] == natural_line[None, :]).astype(BF)
    order_side = (place[:, None] == natural_side[None, :]).astype(BF)
    order_across = (natural_side[:, None] == natural_line[None, :]).astype(BF)
    a0_quarter, a0_got, a1_line, m0_near, order_line, order_side, order_across, vector_rows, own_cotangent = fence(
        a0_quarter, a0_got, a1_line, m0_near, order_line, order_side, order_across, vector_rows, own_cotangent
    )

    a0_across = plane_second(a0_got)
    a0_quarter_other, a0_got_other = core_swap(a0_quarter), (core_swap(a0_got[0]), core_swap(a0_got[1]))
    a1_quarter = line_rows(*a1_line)
    a1_got = plane_first(a1_quarter)
    segment_rows = vector_rows[:, 12 * shard :].astype(jnp.int32)
    pack_segments = take(segment_rows, rank // PACK_DEVS, PACK_DEVS, 0).reshape(-1)
    vector_rows = vector_rows[:, : 12 * shard]
    vector_other = core_swap(vector_rows)
    layer_vectors = []
    for layer in range(2):
        rows = jnp.where(core == layer, vector_rows, vector_other)
        model = jnp.stack([rows[:, i * shard : (i + 1) * shard].reshape(width) for i in range(6)])
        norm_one, rest = dot(model[:2], order_line), dot(model[2:], order_side)
        qv = rows[:, 6 * shard : 8 * shard].reshape(2 * width).astype(F32)
        fc = rows[:, 8 * shard : 12 * shard].reshape(hidden).astype(F32)
        fc = lax.dynamic_slice_in_dim(fc, core * (hidden // 2) + pair_bit * (hidden // 4), hidden // 4, 0)
        qkv = jnp.concatenate([qv[:width], jnp.zeros((width,), F32), qv[width:]])
        layer_vectors.append(((norm_one[0], norm_one[1]), (rest[0], rest[1], rest[2], rest[3]), qkv, fc))
    first_in = reorder(own_inputs, order_side).astype(F32)
    first_line = reorder(own_inputs, order_line).astype(F32)
    first_normed, first_norm_one = attn_in(0, first_line)
    second_up_low = reorder(own_cotangent, order_side)
    second_up_all = gather_tokens(second_up_low)
    (
        a0_across,
        a0_quarter_other,
        a0_got_other,
        a1_quarter,
        a1_got,
        first_normed,
        second_up_low,
        second_up_all,
        m0,
        m0_near,
        m1_yours,
    ) = fence(
        a0_across,
        a0_quarter_other,
        a0_got_other,
        a1_quarter,
        a1_got,
        first_normed,
        second_up_low,
        second_up_all,
        m0,
        m0_near,
        m1_yours,
    )

    mlp_first = gather_side(m0, m0_near)
    a1_across = plane_second(a1_got)
    a0_across_other = [core_swap(part) for part in a0_across]
    attn_first = (
        plane_whole(a0_quarter, a0_got, a0_across),
        plane_whole(a0_quarter_other, a0_got_other, a0_across_other),
    )
    sent = attn_qkv(0, first_normed, *attn_first)
    sent, a1_across, m1_yours = fence(sent, a1_across, m1_yours)

    m1_near = chip_swap(m1_yours, 4)
    first_heads = pack_exchange(sent)
    first_ctx, first_probs = attn_mix(first_heads)
    attn_second = plane_whole(a1_quarter, a1_got, a1_across)
    attn_second = attn_second, tuple(core_swap(part) for part in attn_second)
    first_context, first_middle, first_normed_two, first_norm_two = attn_out(0, first_in, first_ctx, *attn_first)
    first_normed_two, mlp_first, m1, m1_near = fence(first_normed_two, mlp_first, m1, m1_near)
    mlp_second = gather_side(m1, m1_near)
    first_normed_two = gather_tokens(first_normed_two)
    mlp_first = mlp_first[:, :small], mlp_first[:, small:]
    first_out, first_pre, first_act = mlp(0, first_middle, first_normed_two, *mlp_first)
    first_low = first_out.astype(BF)
    second_in = first_low.astype(F32)
    second_line = reorder(first_low, order_across).astype(F32)
    second_normed, second_norm_one = attn_in(1, second_line)
    second_heads = pack_exchange(attn_qkv(1, second_normed, *attn_second))
    second_ctx, second_probs = attn_mix(second_heads)
    second_ctx, mlp_second = fence(second_ctx, mlp_second)
    second_context, second_middle, second_normed_two, second_norm_two = attn_out(1, second_in, second_ctx, *attn_second)
    second_normed_two = gather_tokens(second_normed_two)
    mlp_second = mlp_second[:, :small], mlp_second[:, small:]
    second_out, second_pre, second_act = mlp(1, second_middle, second_normed_two, *mlp_second)
    second_low = second_out.astype(BF)

    second_up = second_up_low.astype(F32)
    second_pre_grad, part = mlp_back(second_up_all, second_pre, *mlp_second)
    second_pre_grad, part = fence(second_pre_grad, part)
    grad_norm = reduce_tokens(part)
    f1_terms = owner_terms(side_by_owner(second_normed_two), second_pre_grad)
    p1_terms = owner_terms(side_by_owner(second_up_all), second_act)
    grad_norm, f1_terms, p1_terms = fence(grad_norm, f1_terms, p1_terms)
    f1_sum, p1_sum = plane_sum(f1_terms), plane_sum(p1_terms)
    second_mid_grad, second_da, attn_mine, attn_yours, heads_grad, second_gain_two, second_bias_two = attn_out_back(
        second_up, grad_norm, second_norm_two, *attn_second
    )
    back = pack_exchange(attend_back(second_heads, second_probs, heads_grad))
    second_grad, second_packed, qkv_mine, qkv_yours, second_gain_one, second_bias_one = attn_qkv_back(
        back, second_mid_grad, second_norm_one, *attn_second
    )
    second_grad_low = second_grad.astype(BF)
    first_up_low = reorder_back(second_grad_low, order_across)
    first_up_low, qkv_mine, qkv_yours = fence(first_up_low, qkv_mine, qkv_yours)
    first_up = first_up_low.astype(F32)
    first_up_all = gather_tokens(first_up_low)
    normed_both, context_both, qkv_both, attn_both = attn_factors(
        second_normed, second_context, qkv_mine, qkv_yours, attn_mine, attn_yours
    )
    a1_terms = owner_terms(
        line_by_owner(jnp.concatenate([normed_both, context_both], axis=0)), beside(qkv_both, attn_both)
    )
    first_up_all, a1_terms, f1_sum = fence(first_up_all, a1_terms, f1_sum)
    a1_sum = plane_sum(a1_terms)
    first_pre_grad, part = mlp_back(first_up_all, first_pre, *mlp_first)
    first_pre_grad, part = fence(first_pre_grad, part)
    grad_norm = reduce_tokens(part)
    f0_terms = owner_terms(side_by_owner(first_normed_two), first_pre_grad)
    p0_terms = owner_terms(side_by_owner(first_up_all), first_act)
    grad_norm, f0_terms, p0_terms, p1_sum = fence(grad_norm, f0_terms, p0_terms, p1_sum)
    f0_sum, p0_sum = plane_sum(f0_terms), plane_sum(p0_terms)
    first_mid_grad, first_da, attn_mine, attn_yours, heads_grad, first_gain_two, first_bias_two = attn_out_back(
        first_up, grad_norm, first_norm_two, *attn_first
    )
    heads_grad, first_mid_grad, attn_mine, attn_yours, f1_sum, p1_sum = fence(
        heads_grad, first_mid_grad, attn_mine, attn_yours, f1_sum, p1_sum
    )
    def by_section(first, second):
        own = jnp.where(core == 0, first, second)
        got = core_swap(jnp.where(core == 0, second, first))
        return ordered(core, own[None], got[None], 0)

    back = pack_exchange(attend_back(first_heads, first_probs, heads_grad))
    section_outputs = by_section(reorder_back(first_low, order_side), reorder_back(second_low, order_side))
    second_vectors = vector_grads(
        second_gain_one,
        second_bias_one,
        second_da,
        second_gain_two,
        second_bias_two,
        second_up_low,
        second_packed,
        second_pre_grad,
    )
    back, section_outputs, second_vectors, f1_sum, p1_sum = fence(
        back, section_outputs, second_vectors, f1_sum, p1_sum
    )
    m1_pieces = line_pieces((f1_sum, p1_sum), False)
    m1_got = line_sum_first(m1_pieces)
    first_grad, first_packed, qkv_mine, qkv_yours, first_gain_one, first_bias_one = attn_qkv_back(
        back, first_mid_grad, first_norm_one, *attn_first
    )
    first_grad_low = first_grad.astype(BF)
    normed_both, context_both, qkv_both, attn_both = attn_factors(
        first_normed, first_context, qkv_mine, qkv_yours, attn_mine, attn_yours
    )
    a0_left = line_terms(normed_both, qkv_both[:, :width])
    a0_right = line_terms(
        jnp.concatenate([normed_both, context_both], axis=0), beside(qkv_both[:, width:], attn_both)
    )
    a0_left, a0_right, first_grad_low, m1_got, a1_sum = fence(a0_left, a0_right, first_grad_low, m1_got, a1_sum)
    a0_got = sum_first(a0_left, a0_right)
    a1_pieces = line_pieces((a1_sum,), True)
    a1_got = line_sum_first(a1_pieces)
    a0_got, a1_got, f0_sum, p0_sum, first_grad_low, first_packed = fence(
        a0_got, a1_got, f0_sum, p0_sum, first_grad_low, first_packed
    )
    first_vectors = vector_grads(
        first_gain_one,
        first_bias_one,
        first_da,
        first_gain_two,
        first_bias_two,
        first_up_low,
        first_packed,
        first_pre_grad,
    )
    vector_rows = jnp.where(core == 0, first_vectors, second_vectors) + core_swap(
        jnp.where(core == 0, second_vectors, first_vectors)
    )
    a0_last = sum_second(a0_left, a0_right, a0_got)
    m0_pieces = line_pieces((f0_sum, p0_sum), False)
    m0_got = line_sum_first(m0_pieces)
    input_grads = by_section(
        reorder_back(first_grad_low, order_line), reorder_back(second_grad_low, order_line)
    )
    a0_last, m0_got, input_grads, vector_rows = fence(a0_last, m0_got, input_grads, vector_rows)
    vector_own = reduce_vector(vector_rows)
    a0_pieces = line_pieces(sum_whole(a0_left, a0_right, a0_last), True)
    a0_got = line_sum_first(a0_pieces)

    def matrix_grads(attn_pieces, attn_got, mlp_pieces, mlp_got):
        same, other = line_sum_whole(attn_pieces, attn_got)
        attn = same + other
        same, other = line_sum_whole(mlp_pieces, mlp_got)
        return (
            attn[:, :qkv_half],
            attn[:, qkv_half:],
            ordered(pair_bit, same[:, :small], other[:, :small], 1),
            ordered(pair_bit, same[:, small:], other[:, small:], 1),
        )

    first_mats = matrix_grads(a0_pieces, a0_got, m0_pieces, m0_got)
    second_mats = matrix_grads(a1_pieces, a1_got, m1_pieces, m1_got)
    mats = []
    for first, second in zip(first_mats, second_mats):
        own = jnp.where(core == 0, first, second)
        got = core_swap(jnp.where(core == 0, second, first))
        mats.append(ordered(core, own, got, 1))
    model = [vector_own[i * shard : (i + 1) * shard] for i in range(6)]
    return (
        section_outputs[None],
        input_grads[None],
        model[0][None],
        model[1][None],
        mats[0][None],
        vector_own[6 * shard : 8 * shard][None],
        mats[1][None],
        model[2][None],
        model[3][None],
        model[4][None],
        mats[2][None],
        vector_own[8 * shard :][None],
        mats[3][None],
        model[5][None],
    )


def solution(mesh):
    in_specs = (
        P(None, "fsdp", None),
        P(None, "fsdp", None),
        P(None, "fsdp"),
        P("section", "fsdp"),
        P("section", "fsdp"),
        P("section", "fsdp", None),
        P("section", "fsdp"),
        P("section", "fsdp", None),
        P("section", "fsdp"),
        P("section", "fsdp"),
        P("section", "fsdp"),
        P("section", "fsdp", None),
        P("section", "fsdp"),
        P("section", "fsdp", None),
        P("section", "fsdp"),
    )
    out_specs = (
        P("section", None, "fsdp", None),
        P("section", None, "fsdp", None),
        P("section", "fsdp"),
        P("section", "fsdp"),
        P("section", "fsdp", None),
        P("section", "fsdp"),
        P("section", "fsdp", None),
        P("section", "fsdp"),
        P("section", "fsdp"),
        P("section", "fsdp"),
        P("section", "fsdp", None),
        P("section", "fsdp"),
        P("section", "fsdp", None),
        P("section", "fsdp"),
    )
    return jax.shard_map(
        on_device, mesh=mesh, in_specs=in_specs, out_specs=out_specs, check_vma=False
    )
```
